32 devices in a mesh: dp: 4 (over y, x), wide: 4 (over z), narrow: 2 (over core).
Axes of the slice: x: 2, y: 2, z: 4, core: 2. Of those that a mesh axis runs over, the one named last changes fastest.
Arguments:
- grad_parts: bfloat16 [8, 32, 73728], P(('dp', 'narrow'), 'wide'), may hold values from -8 to 8
- weight: bfloat16 [32, 73728], P('wide', ('dp', 'narrow')), may hold values from -12 to 12
- row_state: float32 [32], P('wide'), may hold values from 0.01 to 1
- col_state: float32 [73728], P(('dp', 'narrow')), may hold values from 0.01 to 1
Outputs:
- update: float32 [32, 73728], P('wide', ('dp', 'narrow'))
- new_row_state: float32 [32], P('wide')
- new_col_state: float32 [73728], P(('dp', 'narrow'))
The draws below stay inside these ranges and needn't reach their ends.
All inputs are finite; a program needn't handle non-finite values.
Results may differ from the reference program's by a relative error of at most 0.0003.
Values sent between devices are 32-bit elements; how exact they have to be, the bound alone decides.
No kernel may reach another device: no remote copies, remote signals or barrier semaphores. Data moves between devices by JAX's collectives and lax.ppermute only.
A program may use at most 64 MiB of HBM per device.

```python
import math
import jax
import jax.numpy as jnp
from jax import lax

FF = 73728
STEP = 100
ROWS = 32
REPLICAS = 8


def spread_scales(key, count, spread):
    position = jnp.arange(count, dtype=jnp.float32) / count
    rough = jnp.exp(jax.random.uniform(key, (count,), jnp.float32, 0.0, jnp.log(spread)))
    return 3.0 ** position * rough


def draw_grad_parts(key, part):
    key = jax.random.fold_in(key, 11)
    key_rows, key_cols, key_own = jax.random.split(key, 3)
    cols = spread_scales(key_cols, FF, 3.4)
    rows = spread_scales(key_rows, ROWS, 3.4)
    base = jnp.clip(jax.random.normal(key_own, (REPLICAS, ROWS, FF), jnp.float32), -4.0, 4.0)
    factor = 0.1 / jnp.sqrt(jnp.float32(REPLICAS))
    values = jnp.clip(factor * base * rows[None, :, None] * cols[None, None, :], -8.0, 8.0)
    return values.astype(jnp.bfloat16)


def draw_weight(key, part):
    key = jax.random.fold_in(key, 23)
    key_rows, key_cols, key_vals = jax.random.split(key, 3)
    cols = spread_scales(key_cols, FF, 3.4)
    rows = spread_scales(key_rows, ROWS, 3.4)
    base = jnp.clip(jax.random.normal(key_vals, (ROWS, FF), jnp.float32), -4.0, 4.0)
    values = jnp.clip(0.05 * base * rows[:, None] * cols[None, :], -12.0, 12.0)
    return values.astype(jnp.bfloat16)


def block_levels(stream_key, dims, cuts, smallest, high):
    def one(dim, blocks):
        draws = jax.random.uniform(jax.random.fold_in(jax.random.fold_in(stream_key, 6), dim), (blocks,), jnp.float32, smallest / len(cuts), high / len(cuts))
        return jnp.repeat(jnp.exp(draws), dims[dim] // blocks).reshape((-1,) + (1,) * (len(dims) - dim - 1))

    factor_of = one(*cuts[0])
    for cut in cuts[1:]:
        factor_of = factor_of * one(*cut)
    return factor_of


def setup_inputs(seed: int = 0) -> dict:
    arg_keys = jax.random.split(jax.random.key(seed), 5)
    grad_parts = draw_grad_parts(jax.random.fold_in(arg_keys[4], 71), 0)
    weight = draw_weight(jax.random.fold_in(arg_keys[4], 71), 0)
    row_state = jnp.clip(jnp.exp(math.log(1.0) - 4.6051702 * jax.random.uniform(arg_keys[2], (ROWS,), jnp.float32) ** block_levels(arg_keys[2], (ROWS,), ((0, 4),), -0.2, 0.2)), 0.01, 1.0)
    col_state = jnp.clip(jnp.exp(math.log(1.0) - 4.6051702 * jax.random.uniform(arg_keys[3], (FF,), jnp.float32) ** block_levels(arg_keys[3], (FF,), ((0, 8),), -0.2, 0.2)), 0.01, 1.0)
    return {"grad_parts": grad_parts, "weight": weight, "row_state": row_state, "col_state": col_state}


def reference(grad_parts, weight, row_state, col_state):

    def accumulate(total, piece):
        return (total + piece.astype(jnp.float32), None)
    grad, _ = lax.scan(accumulate, jnp.zeros((ROWS, FF), jnp.float32), grad_parts)
    square = grad * grad + 1e-30
    row_mean = lax.optimization_barrier(jnp.mean(square, axis=1))
    col_mean = lax.optimization_barrier(jnp.mean(square, axis=0))
    beta = 1.0 - STEP ** (-0.8)
    new_row_state = beta * row_state + (1.0 - beta) * row_mean
    new_col_state = beta * col_state + (1.0 - beta) * col_mean
    factor = new_row_state[:, None] * new_col_state[None, :]
    scaled = grad / jnp.sqrt(factor)
    clip = jnp.maximum(1.0, jnp.sqrt(jnp.mean(scaled * scaled)))
    weight_f = weight.astype(jnp.float32)
    weight_rms = jnp.maximum(0.001, jnp.sqrt(jnp.mean(weight_f * weight_f)))
    update = weight_rms * scaled / clip
    return (update, new_row_state, new_col_state)
```

```python
import jax
import jax.numpy as jnp
from jax import lax
from jax.experimental import pallas as pl
from jax.experimental.pallas import tpu as pltpu
from jax.sharding import PartitionSpec as P

FF = 73728
STEP = 100
BETA = 1.0 - STEP ** (-0.8)
LANES = 128
VMEM = pl.BlockSpec(memory_space=pltpu.VMEM)
HBM = pl.BlockSpec(memory_space=pltpu.HBM)


def bits_of(size):
    return [1 << b for b in range(size.bit_length() - 1)]


def send_to(x, axes, size, target):
    return lax.ppermute(x, axes, [(i, target(i)) for i in range(size)])


def wide_masks(wide):
    bits = bits_of(wide)
    return [now[:0:-1] + [sum(now)] * (len(now) - 1) + now[:1] for now in (bits[i : i + 2] for i in range(0, len(bits), 2))]


def tree(terms):
    while len(terms) > 1:
        terms = [sum(terms[i : i + 2][1:], terms[i]) for i in range(0, len(terms), 2)]
    return terms[0]


def iota(rows, axis):
    return lax.broadcasted_iota(jnp.int32, (rows, LANES), axis)


def to_lanes(column, first):
    rows = column.shape[0]
    return jnp.sum(jnp.where(iota(rows, 1) == iota(rows, 0) + first, column, 0.0), axis=0, keepdims=True)


def call(kernel, out_shapes, in_specs, *args, out_specs=None, scratch=()):
    return pl.pallas_call(
        kernel,
        out_shape=[jax.ShapeDtypeStruct(shape, jnp.float32) for shape in out_shapes],
        in_specs=in_specs,
        out_specs=out_specs or [VMEM] * len(out_shapes),
        scratch_shapes=scratch,
        compiler_params=pltpu.CompilerParams(vmem_limit_bytes=32 << 20),
    )(*args)


class Blocks:
    def __init__(self, dp, narrow, cols):
        self.narrow, self.cols = narrow, cols
        self.masks = bits_of(dp * narrow)[1:]
        tiles = cols // LANES
        cut = (tiles * 2 + 2) // 3 * LANES
        self.chunks = [(0, cut), (cut, cols - cut)]
        self.keys = [(t, c) for t in range(dp * narrow // 2) for c in range(2)]

    def width(self, key):
        return self.chunks[key[-1]][1]

    def home(self, t):
        steps = len(self.masks)
        return self.side(next((s for s in range(steps) if t >> s & 1), steps))

    def side(self, s):
        return (len(self.masks) - s + 1) & 1

    def mask(self, core, s):
        return self.masks[-1 - s] if core else self.masks[s]

    def target(self, device, s):
        return device ^ self.mask((device ^ self.side(s)) & 1, s) ^ 1

    def start(self, key):
        j, t, c = key
        group = lax.axis_index("dp") * self.narrow + lax.axis_index("narrow")
        group = group ^ j
        reach = [sum(self.mask(core, s) for s in range(len(self.masks)) if t >> s & 1) for core in range(2)]
        block = group ^ jnp.where(group % 2 == 1, reach[1], reach[0])
        return pl.multiple_of(block * self.cols + self.chunks[c][0], LANES)

    def places(self, keys):
        at, out = 0, []
        for key in keys:
            out.append(at)
            at += self.width(key)
        return out, at


def fetch_kernel(blocks, keys, part, out, raw, sem):
    spans = [pl.ds(at, blocks.width(key)) for key, at in zip(keys, blocks.places(keys)[0])]
    copies = [
        pltpu.make_async_copy(part.at[:, pl.ds(blocks.start(key), span.size)], raw.at[:, span], sem.at[i])
        for i, (key, span) in enumerate(zip(keys, spans))
    ]
    for copy in copies:
        copy.start()
    for copy, span in zip(copies, spans):
        copy.wait()
        out[:, span] = raw[:, span].astype(jnp.float32)


def load(blocks, refs, term, width):
    slot, at = term
    if slot == 0:
        return refs[0][:, pl.ds(blocks.start(at), width)].astype(jnp.float32)
    return refs[slot][:, at : at + width]


def merge_kernel(blocks, plan, *refs):
    out = refs[-1]
    at = 0
    for width, terms in plan:
        out[:, at : at + width] = tree([load(blocks, refs, term, width) for term in terms])
        at += width


def grad_kernel(plan_of, blocks, plan, *refs):
    grad_out, *cols_out = refs[plan_of:]
    at = 0
    for width, terms in plan:
        grad = tree([load(blocks, refs, term, width) for term in terms])
        grad_out[:, at : at + width] = grad
        for col_out in cols_out:
            col_out[:, at : at + width] = jnp.sum(grad * grad + 1e-30, axis=0, keepdims=True)
        at += width
    for col_out in cols_out:
        if col_out.shape[1] > at:
            col_out[:, at:] = jnp.zeros((1, col_out.shape[1] - at), jnp.float32)


def square_kernel(grad_in, col_out, row_out):
    square = grad_in[...] * grad_in[...] + 1e-30
    col_out[...] = jnp.sum(square, axis=0, keepdims=True)
    row_out[...] = to_lanes(jnp.sum(square, axis=1, keepdims=True), 0)


def fixed_kernel(weight, row_state, out, line):
    rows = weight.shape[0]
    squares = []
    for at in range(0, weight.shape[1], LANES):
        piece = weight[:, at : at + LANES].astype(jnp.float32)
        squares.append(piece * piece)
    squares = jnp.sum(tree(squares), keepdims=True)
    line[...] = jnp.zeros_like(line)
    line[:, :rows] = row_state[...]
    first = jnp.logical_and(lax.axis_index("dp") == 0, lax.axis_index("narrow") == 0)
    state = jnp.where(first, pltpu.roll(line[...], 2 * rows, 1), 0.0)
    out[...] = jnp.where(iota(1, 1) == 3 * rows, squares, state)


def column_kernel(state, grad_in, row_in, fixed_in, grad_out, message_out):
    rows = grad_in.shape[0]
    grad = grad_in[...] * lax.rsqrt(state[...])
    grad_out[...] = grad
    quot = jnp.sum(grad * grad, axis=1, keepdims=True)
    message = row_in[...] + fixed_in[...] + to_lanes(quot, rows)
    for i in range(message_out.shape[0]):
        message_out[i] = message


def final_kernel(rows_all, sums_in, grad_in, update_out, row_out, update, row_state, sem):
    rows = grad_in.shape[0]
    outer, wide, inner = sums_in.shape[:3]
    layers = [tree([sums_in[o, z, i] for o in range(outer) for i in range(inner)]) for z in range(wide)]
    total = jnp.concatenate(layers, axis=0)
    lane = iota(wide, 1)
    state = pltpu.roll(total, LANES - 2 * rows, 1)
    quot = pltpu.roll(total, LANES - rows, 1)
    new = jnp.where(lane < rows, BETA * state + (1.0 - BETA) * (total / FF), 1.0)
    update_sum = jnp.sum(jnp.where(lane < rows, quot / new, 0.0), keepdims=True)
    weight_sum = jnp.sum(jnp.where(lane == 3 * rows, total, 0.0), keepdims=True)
    clip = jnp.maximum(1.0, jnp.sqrt(update_sum / (rows_all * FF)))
    weight_rms = jnp.maximum(0.001, jnp.sqrt(weight_sum / (rows_all * FF)))
    own = jnp.sum(jnp.where(iota(wide, 0) == lax.axis_index("wide"), new, 0.0), axis=0, keepdims=True)
    row_state[...] = own[:, :rows]
    copies = [pltpu.make_async_copy(row_state, row_out, sem.at[0]), pltpu.make_async_copy(update, update_out, sem.at[1])]
    copies[0].start()
    column = jnp.sum(jnp.where(iota(rows, 1) == iota(rows, 0), own, 0.0), axis=1, keepdims=True)
    update[...] = grad_in[...] * (lax.rsqrt(column) * (weight_rms / clip))
    copies[1].start()
    for copy in copies:
        copy.wait()


def on_device(dp, wide, narrow, grad_parts, weight, row_state, col_state):
    part = grad_parts[0]
    rows, cols = weight.shape
    rows_all = rows * wide
    blocks = Blocks(dp, narrow, cols)
    group_axes = ("dp", "narrow")
    size = dp * narrow
    arrays = [part]
    held = {(t, c): [(0, (blocks.home(t), t, c))] for t, c in blocks.keys}

    def merge(kernel, widths, sums, shapes):
        used = [0] + sorted({slot for terms in sums for slot, _ in terms} - {0}, reverse=True)
        plan = [(width, [(used.index(slot), at) for slot, at in terms]) for width, terms in zip(widths, sums)]
        return call(lambda *refs: kernel(blocks, plan, *refs), shapes, [VMEM] * len(used), *[arrays[u] for u in used])

    def pack(keys, sums):
        return merge(merge_kernel, [blocks.width(key) for key in keys], sums, [(rows, blocks.places(keys)[1])])[0]

    def fetch(keys):
        shape = (rows, blocks.places(keys)[1])
        return call(
            lambda *refs: fetch_kernel(blocks, keys, *refs),
            [shape],
            [HBM],
            pltpu.with_memory_space_constraint(part, pltpu.HBM),
            scratch=[pltpu.VMEM(shape, part.dtype), pltpu.SemaphoreType.DMA((len(keys),))],
        )[0]

    def receive(keys, send, target):
        arrays.append(send_to(send, group_axes, size, target))
        return [(key, (len(arrays) - 1, at)) for key, at in zip(keys, blocks.places(keys)[0])]

    def other(device):
        return device ^ 1

    groups = (
        [key for key in held if key[1] == 0 and key[0] & 1],
        [key for key in held if key[1] == 1],
        [key for key in held if key[1] == 0 and not key[0] & 1],
    )
    for i, keys in enumerate(groups):
        given = [(1 ^ blocks.home(t), t, c) for t, c in keys]
        send = pack(keys, [[(0, key)] for key in given]) if i else fetch(given)
        for key, term in receive(keys, send, other):
            held[key].append(term)
    for s in range(len(blocks.masks)):
        for c in range(2):
            keys = [key for key in held if key[0] >> s & 1 and key[1] == c]
            got = receive(keys, pack(keys, [held.pop(key) for key in keys]), lambda i: blocks.target(i, s))
            got = [((t ^ 1 << s, c), term) for (t, c), term in got]
            away = [(key, term) for key, term in got if blocks.home(key[0]) != blocks.side(s + 1)]
            if away:
                keys = [key for key, _ in away]
                got = [pair for pair in got if pair not in away]
                got += receive(keys, pack(keys, [[term] for _, term in away]), other)
            for key, term in got:
                held[key].append(term)
    left = sorted(held)
    first, *rounds = wide_masks(wide)
    inputs = 1 + len({slot for key in left for slot, _ in held[key]} - {0})
    grad, *sends = merge(
        lambda *refs: grad_kernel(inputs, *refs),
        [blocks.width(key) for key in left],
        [held[key] for key in left],
        [(rows, cols)] + [(1, cols + LANES * (len(first) - 1 - i)) for i in range(len(first))],
    )

    def send_wide(x, mask):
        return send_to(x, ("wide", "narrow"), wide * narrow, lambda i: i ^ mask)

    terms = [send_wide(x, mask * narrow ^ 1)[:, :cols] for x, mask in zip(sends, first)]
    grad = send_to(grad, group_axes, size, other)
    col_sum, row_part = call(square_kernel, [(1, cols), (1, LANES)], [VMEM], grad)
    col_sum = tree(terms + [col_sum])
    for masks in rounds:
        col_sum = tree([send_wide(col_sum, mask * narrow) for mask in masks] + [col_sum])
    new_col_state = BETA * col_state[None] + (1.0 - BETA) * (col_sum / rows_all)
    fixed = call(
        fixed_kernel,
        [(1, LANES)],
        [VMEM] * 2,
        weight, row_state[None],
        scratch=[pltpu.VMEM((1, LANES), jnp.float32)],
    )[0]

    single = dp * wide * narrow <= 64
    group = dp * narrow * (wide if single else 1)
    grad, message = call(
        column_kernel,
        [(rows, cols), (group, 1, LANES)],
        [VMEM] * 4,
        new_col_state, grad, row_part, fixed,
    )
    if single:
        sums = lax.all_to_all(message, ("dp", "wide", "narrow"), 0, 0)
        sums = sums.reshape(dp, wide, narrow, 1, LANES)
    else:
        sums = jnp.sum(lax.all_to_all(message, ("dp", "narrow"), 0, 0), axis=0)
        sums = lax.all_to_all(jnp.broadcast_to(sums, (wide, 1, LANES)), "wide", 0, 0)
        sums = sums.reshape(1, wide, 1, 1, LANES)
    update, new_row_state = call(
        lambda *refs: final_kernel(rows_all, *refs),
        [(rows, cols), (1, rows)],
        [VMEM] * 2,
        sums, grad,
        out_specs=[HBM] * 2,
        scratch=[pltpu.VMEM((rows, cols), jnp.float32), pltpu.VMEM((1, rows), jnp.float32), pltpu.SemaphoreType.DMA((2,))],
    )
    return (update, new_row_state[0], new_col_state[0])


def solution(mesh):
    dp, wide, narrow = (mesh.shape[axis] for axis in ("dp", "wide", "narrow"))

    def body(*args):
        return on_device(dp, wide, narrow, *args)

    return jax.shard_map(
        body,
        mesh=mesh,
        in_specs=(
            P(("dp", "narrow"), "wide", None),
            P("wide", ("dp", "narrow")),
            P("wide"),
            P(("dp", "narrow")),
        ),
        out_specs=(P("wide", ("dp", "narrow")), P("wide"), P(("dp", "narrow"))),
        check_vma=False,
    )
```

```python
import jax
import jax.numpy as jnp
from jax import lax
from jax.experimental import pallas as pl
from jax.experimental.pallas import tpu as pltpu
from jax.sharding import PartitionSpec as P

FF = 73728
STEP = 100
BETA = 1.0 - STEP ** (-0.8)
LANES = 128
PIECES = 2
VMEM = pl.BlockSpec(memory_space=pltpu.VMEM)
HBM = pl.BlockSpec(memory_space=pltpu.HBM)


def bits_of(size):
    return [1 << b for b in range(size.bit_length() - 1)]


def send_to(x, axes, size, target):
    return lax.ppermute(x, axes, [(i, target(i)) for i in range(size)])


def wide_masks(wide):
    bits = bits_of(wide)
    return [[sum(now)] * (len(now) - 1) + now[::-1] for now in (bits[i : i + 2] for i in range(0, len(bits), 2))]


def tree(terms):
    while len(terms) > 1:
        terms = [sum(terms[i : i + 2][1:], terms[i]) for i in range(0, len(terms), 2)]
    return terms[0]


def iota(rows, axis):
    return lax.broadcasted_iota(jnp.int32, (rows, LANES), axis)


def to_lanes(column, first):
    rows = column.shape[0]
    return jnp.sum(jnp.where(iota(rows, 1) == iota(rows, 0) + first, column, 0.0), axis=0, keepdims=True)


def call(kernel, out_shapes, in_specs, *args, scratch=()):
    return pl.pallas_call(
        kernel,
        out_shape=[jax.ShapeDtypeStruct(shape, jnp.float32) for shape in out_shapes],
        in_specs=in_specs,
        out_specs=[VMEM] * len(out_shapes),
        scratch_shapes=scratch,
        compiler_params=pltpu.CompilerParams(vmem_limit_bytes=32 << 20),
    )(*args)


class Blocks:
    def __init__(self, dp, narrow, cols):
        self.narrow, self.cols = narrow, cols
        self.masks = bits_of(dp * narrow)[1:]
        tiles = cols // LANES
        cut = (tiles * 2 + 2) // 3 * LANES
        self.chunks = [(0, cut), (cut, cols - cut)]
        self.keys = [(t, c) for t in range(dp * narrow // 2) for c in range(2)]

    def width(self, key):
        return self.chunks[key[-1]][1]

    def home(self, t):
        steps = len(self.masks)
        return self.side(next((s for s in range(steps) if t >> s & 1), steps))

    def side(self, s):
        return (len(self.masks) - s + 1) & 1

    def mask(self, core, s):
        return self.masks[-1 - s] if core else self.masks[s]

    def target(self, device, s):
        return device ^ self.mask((device ^ self.side(s)) & 1, s) ^ 1

    def start(self, key):
        j, t, c = key
        group = lax.axis_index("dp") * self.narrow + lax.axis_index("narrow")
        group = group ^ j
        reach = [sum(self.mask(core, s) for s in range(len(self.masks)) if t >> s & 1) for core in range(2)]
        block = group ^ jnp.where(group % 2 == 1, reach[1], reach[0])
        return pl.multiple_of(block * self.cols + self.chunks[c][0], LANES)

    def places(self, keys):
        at, out = 0, []
        for key in keys:
            out.append(at)
            at += self.width(key)
        return out, at


def fetch_kernel(blocks, keys, part, out, raw, sem):
    spans, copies = [], []
    for key, at in zip(keys, blocks.places(keys)[0]):
        start, tiles = blocks.start(key), blocks.width(key) // LANES
        cuts = [tiles * i // PIECES * LANES for i in range(PIECES + 1)]
        for a, b in zip(cuts, cuts[1:]):
            spans.append(pl.ds(at + a, b - a))
            source = part.at[:, pl.ds(pl.multiple_of(start + a, LANES), b - a)]
            copies.append(pltpu.make_async_copy(source, raw.at[:, spans[-1]], sem.at[len(copies)]))
    for copy in copies:
        copy.start()
    for copy, span in zip(copies, spans):
        copy.wait()
        out[:, span] = raw[:, span].astype(jnp.float32)


def load(blocks, refs, term, width):
    slot, at = term
    if slot == 0:
        return refs[0][:, pl.ds(blocks.start(at), width)].astype(jnp.float32)
    return refs[slot][:, at : at + width]


def merge_kernel(blocks, plan, *refs):
    out = refs[-1]
    at = 0
    for width, terms in plan:
        out[:, at : at + width] = tree([load(blocks, refs, term, width) for term in terms])
        at += width


def grad_kernel(plan_of, blocks, plan, *refs):
    grad_out, *cols_out = refs[plan_of:]
    at = 0
    for width, terms in plan:
        grad = tree([load(blocks, refs, term, width) for term in terms])
        grad_out[:, at : at + width] = grad
        for col_out in cols_out:
            col_out[:, at : at + width] = jnp.sum(grad * grad + 1e-30, axis=0, keepdims=True)
        at += width
    for col_out in cols_out:
        if col_out.shape[1] > at:
            col_out[:, at:] = jnp.zeros((1, col_out.shape[1] - at), jnp.float32)


def square_kernel(grad_in, col_out, row_out):
    square = grad_in[...] * grad_in[...] + 1e-30
    col_out[...] = jnp.sum(square, axis=0, keepdims=True)
    row_out[...] = to_lanes(jnp.sum(square, axis=1, keepdims=True), 0)


def fixed_kernel(weight, row_state, out, line):
    rows = weight.shape[0]
    squares = []
    for at in range(0, weight.shape[1], LANES):
        piece = weight[:, at : at + LANES].astype(jnp.float32)
        squares.append(piece * piece)
    squares = jnp.sum(tree(squares), keepdims=True)
    line[...] = jnp.zeros_like(line)
    line[:, :rows] = row_state[...]
    first = jnp.logical_and(lax.axis_index("dp") == 0, lax.axis_index("narrow") == 0)
    state = jnp.where(first, pltpu.roll(line[...], 2 * rows, 1), 0.0)
    out[...] = jnp.where(iota(1, 1) == 3 * rows, squares, state)


def column_kernel(state, grad_in, row_in, fixed_in, grad_out, message_out):
    rows = grad_in.shape[0]
    grad = grad_in[...] * lax.rsqrt(state[...])
    grad_out[...] = grad
    quot = jnp.sum(grad * grad, axis=1, keepdims=True)
    message = row_in[...] + fixed_in[...] + to_lanes(quot, rows)
    message_out[...] = jnp.broadcast_to(message, message_out.shape)


def final_kernel(rows_all, wide, inner, sums_in, grad_in, update_out, row_out):
    rows = grad_in.shape[0]
    count = wide * inner
    total = tree([sums_in[i : i + count] for i in range(0, sums_in.shape[0], count)])
    total = tree([pltpu.roll(total, count - k, 0) if k else total for k in range(inner)])
    lane, layer = iota(count, 1), iota(count, 0)
    valid = jnp.logical_and(lane < rows, layer % inner == 0)
    state = pltpu.roll(total, LANES - 2 * rows, 1)
    quot = pltpu.roll(total, LANES - rows, 1)
    new = jnp.where(valid, BETA * state + (1.0 - BETA) * (total / FF), 1.0)
    update_sum = jnp.sum(jnp.where(valid, quot / new, 0.0), keepdims=True)
    weight_sum = jnp.sum(jnp.where(jnp.logical_and(lane == 3 * rows, layer % inner == 0), total, 0.0), keepdims=True)
    clip = jnp.maximum(1.0, jnp.sqrt(update_sum / (rows_all * FF)))
    weight_rms = jnp.maximum(0.001, jnp.sqrt(weight_sum / (rows_all * FF)))
    own = jnp.sum(jnp.where(layer == lax.axis_index("wide") * inner, new, 0.0), axis=0, keepdims=True)
    row_out[...] = own[:, :rows]
    column = jnp.sum(jnp.where(iota(rows, 1) == iota(rows, 0), own, 0.0), axis=1, keepdims=True)
    update_out[...] = grad_in[...] * (lax.rsqrt(column) * (weight_rms / clip))


def on_device(dp, wide, narrow, grad_parts, weight, row_state, col_state):
    part = grad_parts[0]
    rows, cols = weight.shape
    rows_all = rows * wide
    blocks = Blocks(dp, narrow, cols)
    group_axes = ("dp", "narrow")
    size = dp * narrow
    arrays = [part]
    held = {(t, c): [(0, (blocks.home(t), t, c))] for t, c in blocks.keys}

    def merge(kernel, widths, sums, shapes):
        used = [0] + sorted({slot for terms in sums for slot, _ in terms} - {0}, reverse=True)
        plan = [(width, [(used.index(slot), at) for slot, at in terms]) for width, terms in zip(widths, sums)]
        return call(lambda *refs: kernel(blocks, plan, *refs), shapes, [VMEM] * len(used), *[arrays[u] for u in used])

    def pack(keys, sums):
        return merge(merge_kernel, [blocks.width(key) for key in keys], sums, [(rows, blocks.places(keys)[1])])[0]

    def fetch(keys):
        shape = (rows, blocks.places(keys)[1])
        return call(
            lambda *refs: fetch_kernel(blocks, keys, *refs),
            [shape],
            [HBM],
            pltpu.with_memory_space_constraint(part, pltpu.HBM),
            scratch=[pltpu.VMEM(shape, part.dtype), pltpu.SemaphoreType.DMA((PIECES * len(keys),))],
        )[0]

    def receive(keys, send, target):
        arrays.append(send_to(send, group_axes, size, target))
        return [(key, (len(arrays) - 1, at)) for key, at in zip(keys, blocks.places(keys)[0])]

    def other(device):
        return device ^ 1

    groups = (
        [key for key in held if key[1] == 0 and key[0] & 1],
        [key for key in held if key[1] == 1],
        [key for key in held if key[1] == 0 and not key[0] & 1],
    )
    for i, keys in enumerate(groups):
        given = [(1 ^ blocks.home(t), t, c) for t, c in keys]
        send = pack(keys, [[(0, key)] for key in given]) if i else fetch(given)
        for key, term in receive(keys, send, other):
            held[key].append(term)
    for s in range(len(blocks.masks)):
        for c in range(2):
            keys = [key for key in held if key[0] >> s & 1 and key[1] == c]
            got = receive(keys, pack(keys, [held.pop(key) for key in keys]), lambda i: blocks.target(i, s))
            got = [((t ^ 1 << s, c), term) for (t, c), term in got]
            away = [(key, term) for key, term in got if blocks.home(key[0]) != blocks.side(s + 1)]
            if away:
                keys = [key for key, _ in away]
                got = [pair for pair in got if pair not in away]
                got += receive(keys, pack(keys, [[term] for _, term in away]), other)
            for key, term in got:
                held[key].append(term)
    left = sorted(held)
    first, *rounds = wide_masks(wide)
    inputs = 1 + len({slot for key in left for slot, _ in held[key]} - {0})
    grad, *sends = merge(
        lambda *refs: grad_kernel(inputs, *refs),
        [blocks.width(key) for key in left],
        [held[key] for key in left],
        [(rows, cols)] + [(1, cols + LANES * (len(first) - 1 - i)) for i in range(len(first))],
    )

    def send_wide(x, mask):
        return send_to(x, ("wide", "narrow"), wide * narrow, lambda i: i ^ mask)

    terms = [send_wide(x, mask * narrow ^ 1)[:, :cols] for x, mask in zip(sends, first)]
    grad = send_to(grad, group_axes, size, other)
    col_sum, row_part = call(square_kernel, [(1, cols), (1, LANES)], [VMEM], grad)
    col_sum = tree(terms + [col_sum])
    for masks in rounds:
        col_sum = tree([send_wide(col_sum, mask * narrow) for mask in masks] + [col_sum])
    new_col_state = BETA * col_state[None] + (1.0 - BETA) * (col_sum / rows_all)
    fixed = call(
        fixed_kernel,
        [(1, LANES)],
        [VMEM] * 2,
        weight, row_state[None],
        scratch=[pltpu.VMEM((1, LANES), jnp.float32)],
    )[0]

    single = dp * wide * narrow <= 64
    group = dp * narrow * (wide if single else 1)
    grad, message = call(
        column_kernel,
        [(rows, cols), (group, LANES)],
        [VMEM] * 4,
        new_col_state, grad, row_part, fixed,
    )
    if single:
        sums = lax.all_to_all(message, ("dp", "wide", "narrow"), 0, 0, tiled=True)
    else:
        sums = jnp.sum(lax.all_to_all(message, ("dp", "narrow"), 0, 0, tiled=True), axis=0, keepdims=True)
        sums = lax.all_to_all(jnp.broadcast_to(sums, (wide, LANES)), "wide", 0, 0, tiled=True)
    update, new_row_state = call(
        lambda *refs: final_kernel(rows_all, wide, narrow if single else 1, *refs),
        [(rows, cols), (1, rows)],
        [VMEM] * 2,
        sums, grad,
    )
    return (update, new_row_state[0], new_col_state[0])


def solution(mesh):
    dp, wide, narrow = (mesh.shape[axis] for axis in ("dp", "wide", "narrow"))

    def body(*args):
        return on_device(dp, wide, narrow, *args)

    return jax.shard_map(
        body,
        mesh=mesh,
        in_specs=(
            P(("dp", "narrow"), "wide", None),
            P("wide", ("dp", "narrow")),
            P("wide"),
            P(("dp", "narrow")),
        ),
        out_specs=(P("wide", ("dp", "narrow")), P("wide"), P(("dp", "narrow"))),
        check_vma=False,
    )
```

```python
import jax
import jax.numpy as jnp
from jax import lax
from jax.experimental import pallas as pl
from jax.experimental.pallas import tpu as pltpu
from jax.sharding import PartitionSpec as P

FF = 73728
STEP = 100
BETA = 1.0 - STEP ** (-0.8)
LANES = 128
PIECES = 2
VMEM = pl.BlockSpec(memory_space=pltpu.VMEM)
HBM = pl.BlockSpec(memory_space=pltpu.HBM)


def bits_of(size):
    return [1 << b for b in range(size.bit_length() - 1)]


def send_to(x, axes, size, target):
    return lax.ppermute(x, axes, [(i, target(i)) for i in range(size)])


def wide_masks(wide):
    bits = bits_of(wide)
    return [[sum(now)] * (len(now) - 1) + now[::-1] for now in (bits[i : i + 2] for i in range(0, len(bits), 2))]


def tree(terms):
    while len(terms) > 1:
        terms = [sum(terms[i : i + 2][1:], terms[i]) for i in range(0, len(terms), 2)]
    return terms[0]


def iota(rows, axis):
    return lax.broadcasted_iota(jnp.int32, (rows, LANES), axis)


def to_lanes(column, first):
    rows = column.shape[0]
    return jnp.sum(jnp.where(iota(rows, 1) == iota(rows, 0) + first, column, 0.0), axis=0, keepdims=True)


def call(kernel, out_shapes, in_specs, *args, scratch=()):
    return pl.pallas_call(
        kernel,
        out_shape=[jax.ShapeDtypeStruct(shape, jnp.float32) for shape in out_shapes],
        in_specs=in_specs,
        out_specs=[VMEM] * len(out_shapes),
        scratch_shapes=scratch,
        compiler_params=pltpu.CompilerParams(vmem_limit_bytes=32 << 20),
    )(*args)


class Blocks:
    def __init__(self, dp, narrow, cols):
        self.narrow, self.cols = narrow, cols
        self.masks = bits_of(dp * narrow)[1:]
        self.steps = len(self.masks)
        self.all = range(dp * narrow // 2)

    def mask(self, core, s):
        return self.masks[-1 - s] if core else self.masks[s]

    def home(self, t):
        return self.side(next((s for s in range(self.steps) if t >> s & 1), self.steps))

    def side(self, s):
        return (self.steps - s + 1) & 1

    def target(self, device, s, cross):
        return device ^ self.mask((device ^ self.side(s)) & 1, s) ^ cross

    def start(self, j, t):
        group = lax.axis_index("dp") * self.narrow + lax.axis_index("narrow")
        group = group ^ j
        reach = [sum(self.mask(core, s) for s in range(self.steps) if t >> s & 1) for core in range(2)]
        block = group ^ jnp.where(group % 2 == 1, reach[1], reach[0])
        return pl.multiple_of(block * self.cols, LANES)


def fetch_kernel(blocks, keys, part, out, raw, sem):
    spans, copies = [], []
    tiles = blocks.cols // LANES
    cuts = [tiles * i // PIECES * LANES for i in range(PIECES + 1)]
    for i, key in enumerate(keys):
        start = blocks.start(*key)
        for a, b in zip(cuts, cuts[1:]):
            spans.append(pl.ds(i * blocks.cols + a, b - a))
            source = part.at[:, pl.ds(pl.multiple_of(start + a, LANES), b - a)]
            copies.append(pltpu.make_async_copy(source, raw.at[:, spans[-1]], sem.at[len(copies)]))
    for copy in copies:
        copy.start()
    for copy, span in zip(copies, spans):
        copy.wait()
        out[:, span] = raw[:, span].astype(jnp.float32)


def load(blocks, refs, term):
    slot, at = term
    if slot == 0:
        return refs[0][:, pl.ds(blocks.start(*at), blocks.cols)].astype(jnp.float32)
    return refs[slot][:, at * blocks.cols : (at + 1) * blocks.cols]


def merge_kernel(blocks, plan, *refs):
    out = refs[-1]
    for i, terms in enumerate(plan):
        out[:, i * blocks.cols : (i + 1) * blocks.cols] = tree([load(blocks, refs, term) for term in terms])


def grad_kernel(inputs, blocks, plan, *refs):
    grad_out, *cols_out = refs[inputs:]
    cols = blocks.cols
    grad = tree([load(blocks, refs, term) for term in plan[0]])
    grad_out[...] = grad
    col = jnp.sum(grad * grad + 1e-30, axis=0, keepdims=True)
    for col_out in cols_out:
        col_out[:, :cols] = col
        if col_out.shape[1] > cols:
            col_out[:, cols:] = jnp.zeros((1, col_out.shape[1] - cols), jnp.float32)


def square_kernel(grad_in, col_out, row_out):
    square = grad_in[...] * grad_in[...] + 1e-30
    col_out[...] = jnp.sum(square, axis=0, keepdims=True)
    row_out[...] = to_lanes(jnp.sum(square, axis=1, keepdims=True), 0)


def fixed_kernel(weight, row_state, out, line):
    rows = weight.shape[0]
    squares = []
    for at in range(0, weight.shape[1], LANES):
        piece = weight[:, at : at + LANES].astype(jnp.float32)
        squares.append(piece * piece)
    squares = jnp.sum(tree(squares), keepdims=True)
    line[...] = jnp.zeros_like(line)
    line[:, :rows] = row_state[...]
    first = jnp.logical_and(lax.axis_index("dp") == 0, lax.axis_index("narrow") == 0)
    state = jnp.where(first, pltpu.roll(line[...], 2 * rows, 1), 0.0)
    out[...] = jnp.where(iota(1, 1) == 3 * rows, squares, state)


def column_kernel(state, grad_in, row_in, fixed_in, grad_out, message_out):
    rows = grad_in.shape[0]
    grad = grad_in[...] * lax.rsqrt(state[...])
    grad_out[...] = grad
    quot = jnp.sum(grad * grad, axis=1, keepdims=True)
    message = row_in[...] + fixed_in[...] + to_lanes(quot, rows)
    message_out[...] = jnp.broadcast_to(message, message_out.shape)


def final_kernel(rows_all, wide, inner, sums_in, grad_in, update_out, row_out):
    rows = grad_in.shape[0]
    count = wide * inner
    total = tree([sums_in[i : i + count] for i in range(0, sums_in.shape[0], count)])
    total = tree([pltpu.roll(total, count - k, 0) if k else total for k in range(inner)])
    lane, layer = iota(count, 1), iota(count, 0)
    valid = jnp.logical_and(lane < rows, layer % inner == 0)
    state = pltpu.roll(total, LANES - 2 * rows, 1)
    quot = pltpu.roll(total, LANES - rows, 1)
    new = jnp.where(valid, BETA * state + (1.0 - BETA) * (total / FF), 1.0)
    update_sum = jnp.sum(jnp.where(valid, quot / new, 0.0), keepdims=True)
    weight_sum = jnp.sum(jnp.where(jnp.logical_and(lane == 3 * rows, layer % inner == 0), total, 0.0), keepdims=True)
    clip = jnp.maximum(1.0, jnp.sqrt(update_sum / (rows_all * FF)))
    weight_rms = jnp.maximum(0.001, jnp.sqrt(weight_sum / (rows_all * FF)))
    own = jnp.sum(jnp.where(layer == lax.axis_index("wide") * inner, new, 0.0), axis=0, keepdims=True)
    row_out[...] = own[:, :rows]
    column = jnp.sum(jnp.where(iota(rows, 1) == iota(rows, 0), own, 0.0), axis=1, keepdims=True)
    update_out[...] = grad_in[...] * (lax.rsqrt(column) * (weight_rms / clip))


def on_device(dp, wide, narrow, grad_parts, weight, row_state, col_state):
    part = grad_parts[0]
    rows, cols = weight.shape
    rows_all = rows * wide
    blocks = Blocks(dp, narrow, cols)
    group_axes = ("dp", "narrow")
    size = dp * narrow
    arrays = [part]
    held = {t: [(0, (blocks.home(t), t))] for t in blocks.all}

    def merge(kernel, sums, shapes):
        used = [0] + sorted({slot for terms in sums for slot, _ in terms} - {0}, reverse=True)
        plan = [[(used.index(slot), at) for slot, at in terms] for terms in sums]
        return call(lambda *refs: kernel(blocks, plan, *refs), shapes, [VMEM] * len(used), *[arrays[u] for u in used])

    def pack(sums):
        return merge(merge_kernel, sums, [(rows, len(sums) * cols)])[0]

    def fetch(keys):
        shape = (rows, len(keys) * cols)
        return call(
            lambda *refs: fetch_kernel(blocks, keys, *refs),
            [shape],
            [HBM],
            pltpu.with_memory_space_constraint(part, pltpu.HBM),
            scratch=[pltpu.VMEM(shape, part.dtype), pltpu.SemaphoreType.DMA((PIECES * len(keys),))],
        )[0]

    def receive(send, target):
        arrays.append(send_to(send, group_axes, size, target))
        return [(len(arrays) - 1, at) for at in range(send.shape[1] // cols)]

    def other(device):
        return device ^ 1

    def stages(s):
        groups = {}
        for t in blocks.all:
            if t & (2 << s) - 1 == 1 << s:
                cross = blocks.side(s) ^ blocks.home(t ^ 1 << s)
                groups.setdefault((t >> s == 1, 1 - cross), []).append(t)
        return [(ts, 1 - straight) for (_, straight), ts in sorted(groups.items())]

    even = [t for t in blocks.all if t and t % 2 == 0]
    groups = [ts for ts, _ in stages(0)] + [even, [0]]
    for i, ts in enumerate(group for group in groups if group):
        given = [(1 ^ blocks.home(t), t) for t in ts]
        send = pack([[(0, key)] for key in given]) if i else fetch(given)
        for t, term in zip(ts, receive(send, other)):
            held[t].append(term)
    for s in range(blocks.steps):
        for ts, cross in stages(s):
            send = pack([held.pop(t) for t in ts])
            for t, term in zip(ts, receive(send, lambda i: blocks.target(i, s, cross))):
                held[t ^ 1 << s].append(term)
    first, *rounds = wide_masks(wide)
    inputs = 1 + len({slot for slot, _ in held[0]} - {0})
    grad, *sends = merge(
        lambda *refs: grad_kernel(inputs, *refs),
        [held[0]],
        [(rows, cols)] + [(1, cols + LANES * (len(first) - 1 - i)) for i in range(len(first))],
    )

    def send_wide(x, mask):
        return send_to(x, ("wide", "narrow"), wide * narrow, lambda i: i ^ mask)

    terms = [send_wide(x, mask * narrow ^ 1)[:, :cols] for x, mask in zip(sends, first)]
    grad = send_to(grad, group_axes, size, other)
    col_sum, row_part = call(square_kernel, [(1, cols), (1, LANES)], [VMEM], grad)
    col_sum = tree(terms + [col_sum])
    for masks in rounds:
        col_sum = tree([send_wide(col_sum, mask * narrow) for mask in masks] + [col_sum])
    new_col_state = BETA * col_state[None] + (1.0 - BETA) * (col_sum / rows_all)
    fixed = call(
        fixed_kernel,
        [(1, LANES)],
        [VMEM] * 2,
        weight, row_state[None],
        scratch=[pltpu.VMEM((1, LANES), jnp.float32)],
    )[0]

    single = dp * wide * narrow <= 64
    group = dp * narrow * (wide if single else 1)
    grad, message = call(
        column_kernel,
        [(rows, cols), (group, LANES)],
        [VMEM] * 4,
        new_col_state, grad, row_part, fixed,
    )
    if single:
        sums = lax.all_to_all(message, ("dp", "wide", "narrow"), 0, 0, tiled=True)
    else:
        sums = jnp.sum(lax.all_to_all(message, ("dp", "narrow"), 0, 0, tiled=True), axis=0, keepdims=True)
        sums = lax.all_to_all(jnp.broadcast_to(sums, (wide, LANES)), "wide", 0, 0, tiled=True)
    update, new_row_state = call(
        lambda *refs: final_kernel(rows_all, wide, narrow if single else 1, *refs),
        [(rows, cols), (1, rows)],
        [VMEM] * 2,
        sums, grad,
    )
    return (update, new_row_state[0], new_col_state[0])


def solution(mesh):
    dp, wide, narrow = (mesh.shape[axis] for axis in ("dp", "wide", "narrow"))

    def body(*args):
        return on_device(dp, wide, narrow, *args)

    return jax.shard_map(
        body,
        mesh=mesh,
        in_specs=(
            P(("dp", "narrow"), "wide", None),
            P("wide", ("dp", "narrow")),
            P("wide"),
            P(("dp", "narrow")),
        ),
        out_specs=(P("wide", ("dp", "narrow")), P("wide"), P(("dp", "narrow"))),
        check_vma=False,
    )
```

```python
import jax
import jax.numpy as jnp
from jax import lax
from jax.experimental import pallas as pl
from jax.experimental.pallas import tpu as pltpu
from jax.sharding import PartitionSpec as P

FF = 73728
STEP = 100
BETA = 1.0 - STEP ** (-0.8)
LANES = 128
PIECES = 2
VMEM = pl.BlockSpec(memory_space=pltpu.VMEM)
HBM = pl.BlockSpec(memory_space=pltpu.HBM)


def bits_of(size):
    return [1 << b for b in range(size.bit_length() - 1)]


def send_to(x, axes, size, target):
    return lax.ppermute(x, axes, [(i, target(i)) for i in range(size)])


def wide_rounds(wide):
    step, rounds = 1, []
    while step < wide:
        rounds.append((step, min(4, wide // step)))
        step *= rounds[-1][1]
    return rounds


def wide_sum(terms, own):
    return tree(terms[::2] + terms[1::2] + [own])


def tree(terms):
    while len(terms) > 1:
        terms = [sum(terms[i : i + 2][1:], terms[i]) for i in range(0, len(terms), 2)]
    return terms[0]


def iota(rows, axis):
    return lax.broadcasted_iota(jnp.int32, (rows, LANES), axis)


def to_lanes(column, first):
    rows = column.shape[0]
    return jnp.sum(jnp.where(iota(rows, 1) == iota(rows, 0) + first, column, 0.0), axis=0, keepdims=True)


def call(kernel, out_shapes, in_specs, *args, scratch=()):
    return pl.pallas_call(
        kernel,
        out_shape=[jax.ShapeDtypeStruct(shape, jnp.float32) for shape in out_shapes],
        in_specs=in_specs,
        out_specs=[VMEM] * len(out_shapes),
        scratch_shapes=scratch,
        compiler_params=pltpu.CompilerParams(vmem_limit_bytes=32 << 20),
    )(*args)


class Blocks:
    def __init__(self, dp, narrow, cols):
        self.narrow, self.cols = narrow, cols
        self.masks = bits_of(dp * narrow)[1:]
        self.steps = len(self.masks)
        self.all = range(dp * narrow // 2)

    def mask(self, core, s):
        return self.masks[-1 - s] if core else self.masks[s]

    def home(self, t):
        return self.side(next((s for s in range(self.steps) if t >> s & 1), self.steps))

    def side(self, s):
        return (self.steps - s + 1) & 1

    def target(self, device, s, cross):
        return device ^ self.mask((device ^ self.side(s)) & 1, s) ^ cross

    def start(self, j, t):
        group = lax.axis_index("dp") * self.narrow + lax.axis_index("narrow")
        group = group ^ j
        reach = [sum(self.mask(core, s) for s in range(self.steps) if t >> s & 1) for core in range(2)]
        block = group ^ jnp.where(group % 2 == 1, reach[1], reach[0])
        return pl.multiple_of(block * self.cols, LANES)


def fetch_kernel(blocks, keys, part, out, raw, sem):
    spans, copies = [], []
    tiles = blocks.cols // LANES
    cuts = [tiles * i // PIECES * LANES for i in range(PIECES + 1)]
    for i, key in enumerate(keys):
        start = blocks.start(*key)
        for a, b in zip(cuts, cuts[1:]):
            spans.append(pl.ds(i * blocks.cols + a, b - a))
            source = part.at[:, pl.ds(pl.multiple_of(start + a, LANES), b - a)]
            copies.append(pltpu.make_async_copy(source, raw.at[:, spans[-1]], sem.at[len(copies)]))
    for copy in copies:
        copy.start()
    for copy, span in zip(copies, spans):
        copy.wait()
        out[:, span] = raw[:, span].astype(jnp.float32)


def load(blocks, refs, term):
    slot, at = term
    if slot == 0:
        return refs[0][:, pl.ds(blocks.start(*at), blocks.cols)].astype(jnp.float32)
    return refs[slot][:, at * blocks.cols : (at + 1) * blocks.cols]


def merge_kernel(blocks, plan, *refs):
    out = refs[-1]
    for i, terms in enumerate(plan):
        out[:, i * blocks.cols : (i + 1) * blocks.cols] = tree([load(blocks, refs, term) for term in terms])


def grad_kernel(inputs, blocks, plan, *refs):
    grad_out, *cols_out = refs[inputs:]
    cols = blocks.cols
    grad = tree([load(blocks, refs, term) for term in plan[0]])
    grad_out[...] = grad
    col = jnp.sum(grad * grad + 1e-30, axis=0, keepdims=True)
    for col_out in cols_out:
        col_out[:, :cols] = col
        if col_out.shape[1] > cols:
            col_out[:, cols:] = jnp.zeros((1, col_out.shape[1] - cols), jnp.float32)


def square_kernel(grad_in, col_out, row_out):
    square = grad_in[...] * grad_in[...] + 1e-30
    col_out[...] = jnp.sum(square, axis=0, keepdims=True)
    row_out[...] = to_lanes(jnp.sum(square, axis=1, keepdims=True), 0)


def fixed_kernel(weight, row_state, out, line):
    rows = weight.shape[0]
    squares = []
    for at in range(0, weight.shape[1], LANES):
        piece = weight[:, at : at + LANES].astype(jnp.float32)
        squares.append(piece * piece)
    squares = jnp.sum(tree(squares), keepdims=True)
    line[...] = jnp.zeros_like(line)
    line[:, :rows] = row_state[...]
    first = jnp.logical_and(lax.axis_index("dp") == 0, lax.axis_index("narrow") == 0)
    state = jnp.where(first, pltpu.roll(line[...], 2 * rows, 1), 0.0)
    out[...] = jnp.where(iota(1, 1) == 3 * rows, squares, state)


def column_kernel(state, grad_in, row_in, fixed_in, grad_out, message_out):
    rows = grad_in.shape[0]
    grad = grad_in[...] * lax.rsqrt(state[...])
    grad_out[...] = grad
    quot = jnp.sum(grad * grad, axis=1, keepdims=True)
    message = row_in[...] + fixed_in[...] + to_lanes(quot, rows)
    message_out[...] = jnp.broadcast_to(message, message_out.shape)


def final_kernel(rows_all, wide, inner, sums_in, grad_in, update_out, row_out):
    rows = grad_in.shape[0]
    count = wide * inner
    total = tree([sums_in[i : i + count] for i in range(0, sums_in.shape[0], count)])
    total = tree([pltpu.roll(total, count - k, 0) if k else total for k in range(inner)])
    lane, layer = iota(count, 1), iota(count, 0)
    valid = jnp.logical_and(lane < rows, layer % inner == 0)
    state = pltpu.roll(total, LANES - 2 * rows, 1)
    quot = pltpu.roll(total, LANES - rows, 1)
    new = jnp.where(valid, BETA * state + (1.0 - BETA) * (total / FF), 1.0)
    update_sum = jnp.sum(jnp.where(valid, quot / new, 0.0), keepdims=True)
    weight_sum = jnp.sum(jnp.where(jnp.logical_and(lane == 3 * rows, layer % inner == 0), total, 0.0), keepdims=True)
    clip = jnp.maximum(1.0, jnp.sqrt(update_sum / (rows_all * FF)))
    weight_rms = jnp.maximum(0.001, jnp.sqrt(weight_sum / (rows_all * FF)))
    own = jnp.sum(jnp.where(layer == lax.axis_index("wide") * inner, new, 0.0), axis=0, keepdims=True)
    row_out[...] = own[:, :rows]
    column = jnp.sum(jnp.where(iota(rows, 1) == iota(rows, 0), own, 0.0), axis=1, keepdims=True)
    update_out[...] = grad_in[...] * (lax.rsqrt(column) * (weight_rms / clip))


def on_device(dp, wide, narrow, grad_parts, weight, row_state, col_state):
    part = grad_parts[0]
    rows, cols = weight.shape
    rows_all = rows * wide
    blocks = Blocks(dp, narrow, cols)
    group_axes = ("dp", "narrow")
    size = dp * narrow
    arrays = [part]
    held = {t: [(0, (blocks.home(t), t))] for t in blocks.all}

    def merge(kernel, sums, shapes):
        used = [0] + sorted({slot for terms in sums for slot, _ in terms} - {0}, reverse=True)
        plan = [[(used.index(slot), at) for slot, at in terms] for terms in sums]
        return call(lambda *refs: kernel(blocks, plan, *refs), shapes, [VMEM] * len(used), *[arrays[u] for u in used])

    def pack(sums):
        return merge(merge_kernel, sums, [(rows, len(sums) * cols)])[0]

    def fetch(keys):
        shape = (rows, len(keys) * cols)
        return call(
            lambda *refs: fetch_kernel(blocks, keys, *refs),
            [shape],
            [HBM],
            pltpu.with_memory_space_constraint(part, pltpu.HBM),
            scratch=[pltpu.VMEM(shape, part.dtype), pltpu.SemaphoreType.DMA((PIECES * len(keys),))],
        )[0]

    def receive(send, target):
        arrays.append(send_to(send, group_axes, size, target))
        return [(len(arrays) - 1, at) for at in range(send.shape[1] // cols)]

    def other(device):
        return device ^ 1

    def stages(s):
        groups = {}
        for t in blocks.all:
            if t & (2 << s) - 1 == 1 << s:
                cross = blocks.side(s) ^ blocks.home(t ^ 1 << s)
                groups.setdefault((t >> s == 1, 1 - cross), []).append(t)
        return [(ts, 1 - straight) for (_, straight), ts in sorted(groups.items())]

    even = [t for t in blocks.all if t and t % 2 == 0]
    groups = [ts for ts, _ in stages(0)] + [even, [0]]
    for i, ts in enumerate(group for group in groups if group):
        given = [(1 ^ blocks.home(t), t) for t in ts]
        send = pack([[(0, key)] for key in given]) if i else fetch(given)
        for t, term in zip(ts, receive(send, other)):
            held[t].append(term)
    for s in range(blocks.steps):
        for ts, cross in stages(s):
            send = pack([held.pop(t) for t in ts])
            for t, term in zip(ts, receive(send, lambda i: blocks.target(i, s, cross))):
                held[t ^ 1 << s].append(term)
    first, *rounds = wide_rounds(wide)
    inputs = 1 + len({slot for slot, _ in held[0]} - {0})
    grad, *sends = merge(
        lambda *refs: grad_kernel(inputs, *refs),
        [held[0]],
        [(rows, cols)] + [(1, cols + LANES * (first[1] - 1 - k)) for k in range(1, first[1])],
    )

    def send_wide(x, step, width, shift, cross):
        def target(i):
            z, n = divmod(i, narrow)
            place = z // step % width
            z += ((place + shift) % width - place) * step
            return z * narrow + (n ^ cross)

        return send_to(x, ("wide", "narrow"), wide * narrow, target)

    terms = [send_wide(x, *first, k + 1, 1)[:, :cols] for k, x in enumerate(sends)]
    grad = send_to(grad, group_axes, size, other)
    col_sum, row_part = call(square_kernel, [(1, cols), (1, LANES)], [VMEM], grad)
    col_sum = wide_sum(terms, col_sum)
    for step, width in rounds:
        col_sum = wide_sum([send_wide(col_sum, step, width, k, 0) for k in range(1, width)], col_sum)
    new_col_state = BETA * col_state[None] + (1.0 - BETA) * (col_sum / rows_all)
    fixed = call(
        fixed_kernel,
        [(1, LANES)],
        [VMEM] * 2,
        weight, row_state[None],
        scratch=[pltpu.VMEM((1, LANES), jnp.float32)],
    )[0]

    single = dp * wide * narrow <= 64
    group = dp * narrow * (wide if single else 1)
    grad, message = call(
        column_kernel,
        [(rows, cols), (group, LANES)],
        [VMEM] * 4,
        new_col_state, grad, row_part, fixed,
    )
    if single:
        sums = lax.all_to_all(message, ("dp", "wide", "narrow"), 0, 0, tiled=True)
    else:
        sums = jnp.sum(lax.all_to_all(message, ("dp", "narrow"), 0, 0, tiled=True), axis=0, keepdims=True)
        sums = lax.all_to_all(jnp.broadcast_to(sums, (wide, LANES)), "wide", 0, 0, tiled=True)
    update, new_row_state = call(
        lambda *refs: final_kernel(rows_all, wide, narrow if single else 1, *refs),
        [(rows, cols), (1, rows)],
        [VMEM] * 2,
        sums, grad,
    )
    return (update, new_row_state[0], new_col_state[0])


def solution(mesh):
    dp, wide, narrow = (mesh.shape[axis] for axis in ("dp", "wide", "narrow"))

    def body(*args):
        return on_device(dp, wide, narrow, *args)

    return jax.shard_map(
        body,
        mesh=mesh,
        in_specs=(
            P(("dp", "narrow"), "wide", None),
            P("wide", ("dp", "narrow")),
            P("wide"),
            P(("dp", "narrow")),
        ),
        out_specs=(P("wide", ("dp", "narrow")), P("wide"), P(("dp", "narrow"))),
        check_vma=False,
    )
```

```python
import jax
import jax.numpy as jnp
from jax import lax
from jax.experimental import pallas as pl
from jax.experimental.pallas import tpu as pltpu
from jax.sharding import PartitionSpec as P

FF = 73728
STEP = 100
BETA = 1.0 - STEP ** (-0.8)
LANES = 128
VMEM = pl.BlockSpec(memory_space=pltpu.VMEM)


def bits_of(size):
    return [1 << b for b in range(size.bit_length() - 1)]


def send_to(x, axes, size, target):
    return lax.ppermute(x, axes, [(i, target(i)) for i in range(size)])


def wide_masks(wide):
    bits = bits_of(wide)
    return [[sum(now)] * (len(now) - 1) + now[::-1] for now in (bits[i : i + 2] for i in range(0, len(bits), 2))]


def tree(terms):
    while len(terms) > 1:
        terms = [sum(terms[i : i + 2][1:], terms[i]) for i in range(0, len(terms), 2)]
    return terms[0]


def iota(rows, axis):
    return lax.broadcasted_iota(jnp.int32, (rows, LANES), axis)


def to_lanes(column, first):
    rows = column.shape[0]
    return jnp.sum(jnp.where(iota(rows, 1) == iota(rows, 0) + first, column, 0.0), axis=0, keepdims=True)


def call(kernel, out_shapes, in_specs, *args, scratch=()):
    return pl.pallas_call(
        kernel,
        out_shape=[jax.ShapeDtypeStruct(shape, jnp.float32) for shape in out_shapes],
        in_specs=in_specs,
        out_specs=[VMEM] * len(out_shapes),
        scratch_shapes=scratch,
        compiler_params=pltpu.CompilerParams(vmem_limit_bytes=32 << 20),
    )(*args)


class Blocks:
    def __init__(self, dp, narrow, cols):
        self.narrow, self.cols = narrow, cols
        self.masks = bits_of(dp * narrow)[1:]
        self.steps = len(self.masks)
        self.all = range(dp * narrow // 2)

    def mask(self, core, s):
        return self.masks[-1 - s] if core else self.masks[s]

    def home(self, t):
        return self.side(next((s for s in range(self.steps) if t >> s & 1), self.steps))

    def side(self, s):
        return (self.steps - s + 1) & 1

    def target(self, device, s, cross):
        return device ^ self.mask((device ^ self.side(s)) & 1, s) ^ cross

    def start(self, j, t):
        group = lax.axis_index("dp") * self.narrow + lax.axis_index("narrow")
        group = group ^ j
        reach = [sum(self.mask(core, s) for s in range(self.steps) if t >> s & 1) for core in range(2)]
        block = group ^ jnp.where(group % 2 == 1, reach[1], reach[0])
        return pl.multiple_of(block * self.cols, LANES)


def load(blocks, refs, term):
    slot, at = term
    if slot == 0:
        return refs[0][:, pl.ds(blocks.start(*at), blocks.cols)].astype(jnp.float32)
    return refs[slot][:, at * blocks.cols : (at + 1) * blocks.cols]


def merge_kernel(blocks, plan, *refs):
    out = refs[-1]
    for i, terms in enumerate(plan):
        out[:, i * blocks.cols : (i + 1) * blocks.cols] = tree([load(blocks, refs, term) for term in terms])


def grad_kernel(inputs, blocks, plan, *refs):
    grad_out, *cols_out = refs[inputs:]
    cols = blocks.cols
    grad = tree([load(blocks, refs, term) for term in plan[0]])
    grad_out[...] = grad
    col = jnp.sum(grad * grad + 1e-30, axis=0, keepdims=True)
    for col_out in cols_out:
        col_out[:, :cols] = col
        if col_out.shape[1] > cols:
            col_out[:, cols:] = jnp.zeros((1, col_out.shape[1] - cols), jnp.float32)


def square_kernel(grad_in, col_out, row_out):
    square = grad_in[...] * grad_in[...] + 1e-30
    col_out[...] = jnp.sum(square, axis=0, keepdims=True)
    row_out[...] = to_lanes(jnp.sum(square, axis=1, keepdims=True), 0)


def fixed_kernel(weight, row_state, out, line):
    rows = weight.shape[0]
    squares = []
    for at in range(0, weight.shape[1], LANES):
        piece = weight[:, at : at + LANES].astype(jnp.float32)
        squares.append(piece * piece)
    squares = jnp.sum(tree(squares), keepdims=True)
    line[...] = jnp.zeros_like(line)
    line[:, :rows] = row_state[...]
    first = jnp.logical_and(lax.axis_index("dp") == 0, lax.axis_index("narrow") == 0)
    state = jnp.where(first, pltpu.roll(line[...], 2 * rows, 1), 0.0)
    out[...] = jnp.where(iota(1, 1) == 3 * rows, squares, state)


def column_kernel(state, grad_in, row_in, fixed_in, grad_out, message_out):
    rows = grad_in.shape[0]
    grad = grad_in[...] * lax.rsqrt(state[...])
    grad_out[...] = grad
    quot = jnp.sum(grad * grad, axis=1, keepdims=True)
    message = row_in[...] + fixed_in[...] + to_lanes(quot, rows)
    message_out[...] = jnp.broadcast_to(message, message_out.shape)


def final_kernel(rows_all, wide, inner, sums_in, grad_in, update_out, row_out):
    rows = grad_in.shape[0]
    count = wide * inner
    total = tree([sums_in[i : i + count] for i in range(0, sums_in.shape[0], count)])
    total = tree([pltpu.roll(total, count - k, 0) if k else total for k in range(inner)])
    lane, layer = iota(count, 1), iota(count, 0)
    valid = jnp.logical_and(lane < rows, layer % inner == 0)
    state = pltpu.roll(total, LANES - 2 * rows, 1)
    quot = pltpu.roll(total, LANES - rows, 1)
    new = jnp.where(valid, BETA * state + (1.0 - BETA) * (total / FF), 1.0)
    update_sum = jnp.sum(jnp.where(valid, quot / new, 0.0), keepdims=True)
    weight_sum = jnp.sum(jnp.where(jnp.logical_and(lane == 3 * rows, layer % inner == 0), total, 0.0), keepdims=True)
    clip = jnp.maximum(1.0, jnp.sqrt(update_sum / (rows_all * FF)))
    weight_rms = jnp.maximum(0.001, jnp.sqrt(weight_sum / (rows_all * FF)))
    own = jnp.sum(jnp.where(layer == lax.axis_index("wide") * inner, new, 0.0), axis=0, keepdims=True)
    row_out[...] = own[:, :rows]
    column = jnp.sum(jnp.where(iota(rows, 1) == iota(rows, 0), own, 0.0), axis=1, keepdims=True)
    update_out[...] = grad_in[...] * (lax.rsqrt(column) * (weight_rms / clip))


def on_device(dp, wide, narrow, grad_parts, weight, row_state, col_state):
    part = grad_parts[0]
    rows, cols = weight.shape
    rows_all = rows * wide
    blocks = Blocks(dp, narrow, cols)
    group_axes = ("dp", "narrow")
    size = dp * narrow
    arrays = [part]
    held = {t: [(0, (blocks.home(t), t))] for t in blocks.all}

    def merge(kernel, sums, shapes):
        used = [0] + sorted({slot for terms in sums for slot, _ in terms} - {0}, reverse=True)
        plan = [[(used.index(slot), at) for slot, at in terms] for terms in sums]
        return call(lambda *refs: kernel(blocks, plan, *refs), shapes, [VMEM] * len(used), *[arrays[u] for u in used])

    def pack(sums):
        return merge(merge_kernel, sums, [(rows, len(sums) * cols)])[0]

    def receive(send, target):
        arrays.append(send_to(send, group_axes, size, target))
        return [(len(arrays) - 1, at) for at in range(send.shape[1] // cols)]

    def other(device):
        return device ^ 1

    def stages(s):
        groups = {}
        for t in blocks.all:
            if t & (2 << s) - 1 == 1 << s:
                cross = blocks.side(s) ^ blocks.home(t ^ 1 << s)
                groups.setdefault((t >> s == 1, 1 - cross), []).append(t)
        return [(ts, 1 - straight) for (_, straight), ts in sorted(groups.items())]

    even = [t for t in blocks.all if t and t % 2 == 0]
    groups = [ts for ts, _ in stages(0)] + [even, [0]]
    for ts in (group for group in groups if group):
        send = pack([[(0, (1 ^ blocks.home(t), t))] for t in ts])
        for t, term in zip(ts, receive(send, other)):
            held[t].append(term)
    for s in range(blocks.steps):
        for ts, cross in stages(s):
            send = pack([held.pop(t) for t in ts])
            for t, term in zip(ts, receive(send, lambda i: blocks.target(i, s, cross))):
                held[t ^ 1 << s].append(term)
    first, *rounds = wide_masks(wide)
    inputs = 1 + len({slot for slot, _ in held[0]} - {0})
    grad, *sends = merge(
        lambda *refs: grad_kernel(inputs, *refs),
        [held[0]],
        [(rows, cols)] + [(1, cols + LANES * (len(first) - 1 - i)) for i in range(len(first))],
    )

    def send_wide(x, mask):
        return send_to(x, ("wide", "narrow"), wide * narrow, lambda i: i ^ mask)

    terms = [send_wide(x, mask * narrow ^ 1)[:, :cols] for x, mask in zip(sends, first)]
    grad = send_to(grad, group_axes, size, other)
    col_sum, row_part = call(square_kernel, [(1, cols), (1, LANES)], [VMEM], grad)
    col_sum = tree(terms + [col_sum])
    for masks in rounds:
        col_sum = tree([send_wide(col_sum, mask * narrow) for mask in masks] + [col_sum])
    new_col_state = BETA * col_state[None] + (1.0 - BETA) * (col_sum / rows_all)
    fixed = call(
        fixed_kernel,
        [(1, LANES)],
        [VMEM] * 2,
        weight, row_state[None],
        scratch=[pltpu.VMEM((1, LANES), jnp.float32)],
    )[0]

    single = dp * wide * narrow <= 64
    group = dp * narrow * (wide if single else 1)
    grad, message = call(
        column_kernel,
        [(rows, cols), (group, LANES)],
        [VMEM] * 4,
        new_col_state, grad, row_part, fixed,
    )
    if single:
        sums = lax.all_to_all(message, ("dp", "wide", "narrow"), 0, 0, tiled=True)
    else:
        sums = jnp.sum(lax.all_to_all(message, ("dp", "narrow"), 0, 0, tiled=True), axis=0, keepdims=True)
        sums = lax.all_to_all(jnp.broadcast_to(sums, (wide, LANES)), "wide", 0, 0, tiled=True)
    update, new_row_state = call(
        lambda *refs: final_kernel(rows_all, wide, narrow if single else 1, *refs),
        [(rows, cols), (1, rows)],
        [VMEM] * 2,
        sums, grad,
    )
    return (update, new_row_state[0], new_col_state[0])


def solution(mesh):
    dp, wide, narrow = (mesh.shape[axis] for axis in ("dp", "wide", "narrow"))

    def body(*args):
        return on_device(dp, wide, narrow, *args)

    return jax.shard_map(
        body,
        mesh=mesh,
        in_specs=(
            P(("dp", "narrow"), "wide", None),
            P("wide", ("dp", "narrow")),
            P("wide"),
            P(("dp", "narrow")),
        ),
        out_specs=(P("wide", ("dp", "narrow")), P("wide"), P(("dp", "narrow"))),
        check_vma=False,
    )
```

```python
import jax
import jax.numpy as jnp
from jax import lax
from jax.experimental import pallas as pl
from jax.experimental.pallas import tpu as pltpu
from jax.sharding import PartitionSpec as P

FF = 73728
STEP = 100
BETA = 1.0 - STEP ** (-0.8)
LANES = 128
PIECES = 2
VMEM = pl.BlockSpec(memory_space=pltpu.VMEM)
HBM = pl.BlockSpec(memory_space=pltpu.HBM)


def bits_of(size):
    return [1 << b for b in range(size.bit_length() - 1)]


def send_to(x, axes, size, target):
    return lax.ppermute(x, axes, [(i, target(i)) for i in range(size)])


def wide_masks(wide):
    bits = bits_of(wide)
    return [[sum(now)] * (len(now) - 1) + now[::-1] for now in (bits[i : i + 2] for i in range(0, len(bits), 2))]


def tree(terms):
    while len(terms) > 1:
        terms = [sum(terms[i : i + 2][1:], terms[i]) for i in range(0, len(terms), 2)]
    return terms[0]


def iota(rows, axis):
    return lax.broadcasted_iota(jnp.int32, (rows, LANES), axis)


def to_lanes(column, first):
    rows = column.shape[0]
    return jnp.sum(jnp.where(iota(rows, 1) == iota(rows, 0) + first, column, 0.0), axis=0, keepdims=True)


def call(kernel, out_shapes, in_specs, *args, scratch=()):
    return pl.pallas_call(
        kernel,
        out_shape=[jax.ShapeDtypeStruct(shape, jnp.float32) for shape in out_shapes],
        in_specs=in_specs,
        out_specs=[VMEM] * len(out_shapes),
        scratch_shapes=scratch,
        compiler_params=pltpu.CompilerParams(vmem_limit_bytes=32 << 20),
    )(*args)


class Blocks:
    def __init__(self, dp, narrow, cols):
        self.narrow, self.cols = narrow, cols
        self.masks = bits_of(dp * narrow)[1:]
        self.steps = len(self.masks)
        self.all = range(dp * narrow // 2)

    def mask(self, core, s):
        return self.masks[-1 - s] if core else self.masks[s]

    def home(self, t):
        return self.side(next((s for s in range(self.steps) if t >> s & 1), self.steps))

    def side(self, s):
        return (self.steps - s + 1) & 1

    def target(self, device, s, cross):
        return device ^ self.mask((device ^ self.side(s)) & 1, s) ^ cross

    def start(self, j, t):
        group = lax.axis_index("dp") * self.narrow + lax.axis_index("narrow")
        group = group ^ j
        reach = [sum(self.mask(core, s) for s in range(self.steps) if t >> s & 1) for core in range(2)]
        block = group ^ jnp.where(group % 2 == 1, reach[1], reach[0])
        return pl.multiple_of(block * self.cols, LANES)


def fetch_kernel(blocks, keys, part, out, raw, sem):
    spans, copies = [], []
    tiles = blocks.cols // LANES
    cuts = [tiles * i // PIECES * LANES for i in range(PIECES + 1)]
    for i, key in enumerate(keys):
        start = blocks.start(*key)
        for a, b in zip(cuts, cuts[1:]):
            spans.append(pl.ds(i * blocks.cols + a, b - a))
            source = part.at[:, pl.ds(pl.multiple_of(start + a, LANES), b - a)]
            copies.append(pltpu.make_async_copy(source, raw.at[:, spans[-1]], sem.at[len(copies)]))
    for copy in copies:
        copy.start()
    for copy, span in zip(copies, spans):
        copy.wait()
        out[:, span] = raw[:, span].astype(jnp.float32)


def load(blocks, refs, term):
    slot, at = term
    if slot == 0:
        return refs[0][:, pl.ds(blocks.start(*at), blocks.cols)].astype(jnp.float32)
    return refs[slot][:, at * blocks.cols : (at + 1) * blocks.cols]


def merge_kernel(blocks, plan, *refs):
    out = refs[-1]
    for i, terms in enumerate(plan):
        out[:, i * blocks.cols : (i + 1) * blocks.cols] = tree([load(blocks, refs, term) for term in terms])


def grad_kernel(inputs, blocks, plan, *refs):
    grad_out, *cols_out = refs[inputs:]
    cols = blocks.cols
    grad = tree([load(blocks, refs, term) for term in plan[0]])
    grad_out[...] = grad
    col = jnp.sum(grad * grad + 1e-30, axis=0, keepdims=True)
    for col_out in cols_out:
        col_out[:, :cols] = col
        if col_out.shape[1] > cols:
            col_out[:, cols:] = jnp.zeros((1, col_out.shape[1] - cols), jnp.float32)


def fixed_kernel(weight, row_state, out, line):
    rows = weight.shape[0]
    squares = []
    for at in range(0, weight.shape[1], LANES):
        piece = weight[:, at : at + LANES].astype(jnp.float32)
        squares.append(piece * piece)
    squares = jnp.sum(tree(squares), keepdims=True)
    line[...] = jnp.zeros_like(line)
    line[:, :rows] = row_state[...]
    first = jnp.logical_and(lax.axis_index("dp") == 0, lax.axis_index("narrow") == 0)
    state = jnp.where(first, pltpu.roll(line[...], 2 * rows, 1), 0.0)
    out[...] = jnp.where(iota(1, 1) == 3 * rows, squares, state)


def column_kernel(state, grad_in, fixed_in, grad_out, message_out):
    rows = grad_in.shape[0]
    row = jnp.sum(grad_in[...] * grad_in[...] + 1e-30, axis=1, keepdims=True)
    grad = grad_in[...] * lax.rsqrt(state[...])
    grad_out[...] = grad
    quot = jnp.sum(grad * grad, axis=1, keepdims=True)
    message = to_lanes(row, 0) + fixed_in[...] + to_lanes(quot, rows)
    message_out[...] = jnp.broadcast_to(message, message_out.shape)


def final_kernel(rows_all, wide, inner, sums_in, grad_in, update_out, row_out):
    rows = grad_in.shape[0]
    count = wide * inner
    total = tree([sums_in[i : i + count] for i in range(0, sums_in.shape[0], count)])
    total = tree([pltpu.roll(total, count - k, 0) if k else total for k in range(inner)])
    lane, layer = iota(count, 1), iota(count, 0)
    valid = jnp.logical_and(lane < rows, layer % inner == 0)
    state = pltpu.roll(total, LANES - 2 * rows, 1)
    quot = pltpu.roll(total, LANES - rows, 1)
    new = jnp.where(valid, BETA * state + (1.0 - BETA) * (total / FF), 1.0)
    update_sum = jnp.sum(jnp.where(valid, quot / new, 0.0), keepdims=True)
    weight_sum = jnp.sum(jnp.where(jnp.logical_and(lane == 3 * rows, layer % inner == 0), total, 0.0), keepdims=True)
    clip = jnp.maximum(1.0, jnp.sqrt(update_sum / (rows_all * FF)))
    weight_rms = jnp.maximum(0.001, jnp.sqrt(weight_sum / (rows_all * FF)))
    own = jnp.sum(jnp.where(layer == lax.axis_index("wide") * inner, new, 0.0), axis=0, keepdims=True)
    row_out[...] = own[:, :rows]
    column = jnp.sum(jnp.where(iota(rows, 1) == iota(rows, 0), own, 0.0), axis=1, keepdims=True)
    update_out[...] = grad_in[...] * (lax.rsqrt(column) * (weight_rms / clip))


def on_device(dp, wide, narrow, grad_parts, weight, row_state, col_state):
    part = grad_parts[0]
    rows, cols = weight.shape
    rows_all = rows * wide
    blocks = Blocks(dp, narrow, cols)
    group_axes = ("dp", "narrow")
    size = dp * narrow
    arrays = [part]
    held = {t: [(0, (blocks.home(t), t))] for t in blocks.all}

    def merge(kernel, sums, shapes):
        used = [0] + sorted({slot for terms in sums for slot, _ in terms} - {0}, reverse=True)
        plan = [[(used.index(slot), at) for slot, at in terms] for terms in sums]
        return call(lambda *refs: kernel(blocks, plan, *refs), shapes, [VMEM] * len(used), *[arrays[u] for u in used])

    def pack(sums):
        return merge(merge_kernel, sums, [(rows, len(sums) * cols)])[0]

    def fetch(keys):
        shape = (rows, len(keys) * cols)
        return call(
            lambda *refs: fetch_kernel(blocks, keys, *refs),
            [shape],
            [HBM],
            pltpu.with_memory_space_constraint(part, pltpu.HBM),
            scratch=[pltpu.VMEM(shape, part.dtype), pltpu.SemaphoreType.DMA((PIECES * len(keys),))],
        )[0]

    def receive(send, target):
        arrays.append(send_to(send, group_axes, size, target))
        return [(len(arrays) - 1, at) for at in range(send.shape[1] // cols)]

    def other(device):
        return device ^ 1

    def stages(s):
        groups = {}
        for t in blocks.all:
            if t & (2 << s) - 1 == 1 << s:
                cross = blocks.side(s) ^ blocks.home(t ^ 1 << s)
                groups.setdefault((t >> s == 1, 1 - cross), []).append(t)
        return [(ts, 1 - straight) for (_, straight), ts in sorted(groups.items())]

    even = [t for t in blocks.all if t and t % 2 == 0]
    groups = [ts for ts, _ in stages(0)] + [even, [0]]
    for i, ts in enumerate(group for group in groups if group):
        given = [(1 ^ blocks.home(t), t) for t in ts]
        send = pack([[(0, key)] for key in given]) if i else fetch(given)
        for t, term in zip(ts, receive(send, other)):
            held[t].append(term)
    for s in range(blocks.steps):
        for ts, cross in stages(s):
            send = pack([held.pop(t) for t in ts])
            for t, term in zip(ts, receive(send, lambda i: blocks.target(i, s, cross))):
                held[t ^ 1 << s].append(term)
    first, *rounds = wide_masks(wide)
    inputs = 1 + len({slot for slot, _ in held[0]} - {0})
    grad, *sends = merge(
        lambda *refs: grad_kernel(inputs, *refs),
        [held[0]],
        [(rows, cols)] + [(1, cols + LANES * (len(first) - i)) for i in range(len(first) + 1)],
    )

    def send_wide(x, mask):
        return send_to(x, ("wide", "narrow"), wide * narrow, lambda i: i ^ mask)

    terms = [send_wide(x, mask * narrow ^ 1)[:, :cols] for x, mask in zip(sends, first)]
    grad = send_to(grad, group_axes, size, other)
    col_sum = tree(terms + [send_to(sends[-1], group_axes, size, other)])
    for masks in rounds:
        col_sum = tree([send_wide(col_sum, mask * narrow) for mask in masks] + [col_sum])
    new_col_state = BETA * col_state[None] + (1.0 - BETA) * (col_sum / rows_all)
    fixed = call(
        fixed_kernel,
        [(1, LANES)],
        [VMEM] * 2,
        weight, row_state[None],
        scratch=[pltpu.VMEM((1, LANES), jnp.float32)],
    )[0]

    single = dp * wide * narrow <= 64
    group = dp * narrow * (wide if single else 1)
    grad, message = call(
        column_kernel,
        [(rows, cols), (group, LANES)],
        [VMEM] * 3,
        new_col_state, grad, fixed,
    )
    if single:
        sums = lax.all_to_all(message, ("dp", "wide", "narrow"), 0, 0, tiled=True)
    else:
        sums = jnp.sum(lax.all_to_all(message, ("dp", "narrow"), 0, 0, tiled=True), axis=0, keepdims=True)
        sums = lax.all_to_all(jnp.broadcast_to(sums, (wide, LANES)), "wide", 0, 0, tiled=True)
    update, new_row_state = call(
        lambda *refs: final_kernel(rows_all, wide, narrow if single else 1, *refs),
        [(rows, cols), (1, rows)],
        [VMEM] * 2,
        sums, grad,
    )
    return (update, new_row_state[0], new_col_state[0])


def solution(mesh):
    dp, wide, narrow = (mesh.shape[axis] for axis in ("dp", "wide", "narrow"))

    def body(*args):
        return on_device(dp, wide, narrow, *args)

    return jax.shard_map(
        body,
        mesh=mesh,
        in_specs=(
            P(("dp", "narrow"), "wide", None),
            P("wide", ("dp", "narrow")),
            P("wide"),
            P(("dp", "narrow")),
        ),
        out_specs=(P("wide", ("dp", "narrow")), P("wide"), P(("dp", "narrow"))),
        check_vma=False,
    )
```

```python
import jax
import jax.numpy as jnp
from jax import lax
from jax.experimental import pallas as pl
from jax.experimental.pallas import tpu as pltpu
from jax.sharding import PartitionSpec as P

FF = 73728
STEP = 100
BETA = 1.0 - STEP ** (-0.8)
LANES = 128
PIECES = 4
VMEM = pl.BlockSpec(memory_space=pltpu.VMEM)
HBM = pl.BlockSpec(memory_space=pltpu.HBM)


def bits_of(size):
    return [1 << b for b in range(size.bit_length() - 1)]


def send_to(x, axes, size, target):
    return lax.ppermute(x, axes, [(i, target(i)) for i in range(size)])


def wide_masks(wide):
    bits = bits_of(wide)
    return [[sum(now)] * (len(now) - 1) + now[::-1] for now in (bits[i : i + 2] for i in range(0, len(bits), 2))]


def tree(terms):
    while len(terms) > 1:
        terms = [sum(terms[i : i + 2][1:], terms[i]) for i in range(0, len(terms), 2)]
    return terms[0]


def iota(rows, axis):
    return lax.broadcasted_iota(jnp.int32, (rows, LANES), axis)


def to_lanes(column, first):
    rows = column.shape[0]
    return jnp.sum(jnp.where(iota(rows, 1) == iota(rows, 0) + first, column, 0.0), axis=0, keepdims=True)


def call(kernel, out_shapes, in_specs, *args, scratch=()):
    return pl.pallas_call(
        kernel,
        out_shape=[jax.ShapeDtypeStruct(shape, jnp.float32) for shape in out_shapes],
        in_specs=in_specs,
        out_specs=[VMEM] * len(out_shapes),
        scratch_shapes=scratch,
        compiler_params=pltpu.CompilerParams(vmem_limit_bytes=32 << 20),
    )(*args)


class Blocks:
    def __init__(self, dp, narrow, cols):
        self.narrow, self.cols = narrow, cols
        self.masks = bits_of(dp * narrow)[1:]
        self.steps = len(self.masks)
        self.all = range(dp * narrow // 2)

    def mask(self, core, s):
        return self.masks[-1 - s] if core else self.masks[s]

    def home(self, t):
        return self.side(next((s for s in range(self.steps) if t >> s & 1), self.steps))

    def side(self, s):
        return (self.steps - s + 1) & 1

    def target(self, device, s, cross):
        return device ^ self.mask((device ^ self.side(s)) & 1, s) ^ cross

    def start(self, j, t):
        group = lax.axis_index("dp") * self.narrow + lax.axis_index("narrow")
        group = group ^ j
        reach = [sum(self.mask(core, s) for s in range(self.steps) if t >> s & 1) for core in range(2)]
        block = group ^ jnp.where(group % 2 == 1, reach[1], reach[0])
        return pl.multiple_of(block * self.cols, LANES)


def fetch_kernel(blocks, keys, part, out, raw, sem):
    spans, copies = [], []
    tiles = blocks.cols // LANES
    cuts = [tiles * i // PIECES * LANES for i in range(PIECES + 1)]
    for i, key in enumerate(keys):
        start = blocks.start(*key)
        for a, b in zip(cuts, cuts[1:]):
            spans.append(pl.ds(i * blocks.cols + a, b - a))
            source = part.at[:, pl.ds(pl.multiple_of(start + a, LANES), b - a)]
            copies.append(pltpu.make_async_copy(source, raw.at[:, spans[-1]], sem.at[len(copies)]))
    for copy in copies:
        copy.start(priority=1)
    for copy, span in zip(copies, spans):
        copy.wait()
        out[:, span] = raw[:, span].astype(jnp.float32)


def load(blocks, refs, term):
    slot, at = term
    if slot == 0:
        return refs[0][:, pl.ds(blocks.start(*at), blocks.cols)].astype(jnp.float32)
    return refs[slot][:, at * blocks.cols : (at + 1) * blocks.cols]


def merge_kernel(blocks, plan, *refs):
    out = refs[-1]
    for i, terms in enumerate(plan):
        out[:, i * blocks.cols : (i + 1) * blocks.cols] = tree([load(blocks, refs, term) for term in terms])


def grad_kernel(inputs, blocks, plan, *refs):
    grad_out, *cols_out = refs[inputs:]
    cols = blocks.cols
    grad = tree([load(blocks, refs, term) for term in plan[0]])
    grad_out[...] = grad
    col = jnp.sum(grad * grad + 1e-30, axis=0, keepdims=True)
    for col_out in cols_out:
        col_out[:, :cols] = col
        if col_out.shape[1] > cols:
            col_out[:, cols:] = jnp.zeros((1, col_out.shape[1] - cols), jnp.float32)


def fixed_kernel(weight, row_state, out, line):
    rows = weight.shape[0]
    squares = []
    for at in range(0, weight.shape[1], LANES):
        piece = weight[:, at : at + LANES].astype(jnp.float32)
        squares.append(piece * piece)
    squares = jnp.sum(tree(squares), keepdims=True)
    line[...] = jnp.zeros_like(line)
    line[:, :rows] = row_state[...]
    first = jnp.logical_and(lax.axis_index("dp") == 0, lax.axis_index("narrow") == 0)
    state = jnp.where(first, pltpu.roll(line[...], 2 * rows, 1), 0.0)
    out[...] = jnp.where(iota(1, 1) == 3 * rows, squares, state)


def column_kernel(state, grad_in, fixed_in, grad_out, message_out):
    rows = grad_in.shape[0]
    row = jnp.sum(grad_in[...] * grad_in[...] + 1e-30, axis=1, keepdims=True)
    grad = grad_in[...] * lax.rsqrt(state[...])
    grad_out[...] = grad
    quot = jnp.sum(grad * grad, axis=1, keepdims=True)
    message = to_lanes(row, 0) + fixed_in[...] + to_lanes(quot, rows)
    message_out[...] = jnp.broadcast_to(message, message_out.shape)


def final_kernel(rows_all, wide, inner, sums_in, grad_in, update_out, row_out):
    rows = grad_in.shape[0]
    count = wide * inner
    total = tree([sums_in[i : i + count] for i in range(0, sums_in.shape[0], count)])
    total = tree([pltpu.roll(total, count - k, 0) if k else total for k in range(inner)])
    lane, layer = iota(count, 1), iota(count, 0)
    valid = jnp.logical_and(lane < rows, layer % inner == 0)
    state = pltpu.roll(total, LANES - 2 * rows, 1)
    quot = pltpu.roll(total, LANES - rows, 1)
    new = jnp.where(valid, BETA * state + (1.0 - BETA) * (total / FF), 1.0)
    update_sum = jnp.sum(jnp.where(valid, quot / new, 0.0), keepdims=True)
    weight_sum = jnp.sum(jnp.where(jnp.logical_and(lane == 3 * rows, layer % inner == 0), total, 0.0), keepdims=True)
    clip = jnp.maximum(1.0, jnp.sqrt(update_sum / (rows_all * FF)))
    weight_rms = jnp.maximum(0.001, jnp.sqrt(weight_sum / (rows_all * FF)))
    own = jnp.sum(jnp.where(layer == lax.axis_index("wide") * inner, new, 0.0), axis=0, keepdims=True)
    row_out[...] = own[:, :rows]
    column = jnp.sum(jnp.where(iota(rows, 1) == iota(rows, 0), own, 0.0), axis=1, keepdims=True)
    update_out[...] = grad_in[...] * (lax.rsqrt(column) * (weight_rms / clip))


def on_device(dp, wide, narrow, grad_parts, weight, row_state, col_state):
    part = grad_parts[0]
    rows, cols = weight.shape
    rows_all = rows * wide
    blocks = Blocks(dp, narrow, cols)
    group_axes = ("dp", "narrow")
    size = dp * narrow
    arrays = [part]
    held = {t: [(0, (blocks.home(t), t))] for t in blocks.all}

    def merge(kernel, sums, shapes):
        used = [0] + sorted({slot for terms in sums for slot, _ in terms} - {0}, reverse=True)
        plan = [[(used.index(slot), at) for slot, at in terms] for terms in sums]
        return call(lambda *refs: kernel(blocks, plan, *refs), shapes, [VMEM] * len(used), *[arrays[u] for u in used])

    def pack(sums):
        return merge(merge_kernel, sums, [(rows, len(sums) * cols)])[0]

    def fetch(keys):
        shape = (rows, len(keys) * cols)
        return call(
            lambda *refs: fetch_kernel(blocks, keys, *refs),
            [shape],
            [HBM],
            pltpu.with_memory_space_constraint(part, pltpu.HBM),
            scratch=[pltpu.VMEM(shape, part.dtype), pltpu.SemaphoreType.DMA((PIECES * len(keys),))],
        )[0]

    def receive(send, target):
        arrays.append(send_to(send, group_axes, size, target))
        return [(len(arrays) - 1, at) for at in range(send.shape[1] // cols)]

    def other(device):
        return device ^ 1

    def stages(s):
        groups = {}
        for t in blocks.all:
            if t & (2 << s) - 1 == 1 << s:
                cross = blocks.side(s) ^ blocks.home(t ^ 1 << s)
                groups.setdefault((t >> s == 1, 1 - cross), []).append(t)
        return [(ts, 1 - straight) for (_, straight), ts in sorted(groups.items())]

    even = [t for t in blocks.all if t and t % 2 == 0]
    groups = [ts for ts, _ in stages(0)] + [even, [0]]
    for i, ts in enumerate(group for group in groups if group):
        given = [(1 ^ blocks.home(t), t) for t in ts]
        send = pack([[(0, key)] for key in given]) if i else fetch(given)
        for t, term in zip(ts, receive(send, other)):
            held[t].append(term)
    for s in range(blocks.steps):
        for ts, cross in stages(s):
            send = pack([held.pop(t) for t in ts])
            for t, term in zip(ts, receive(send, lambda i: blocks.target(i, s, cross))):
                held[t ^ 1 << s].append(term)
    first, *rounds = wide_masks(wide)
    inputs = 1 + len({slot for slot, _ in held[0]} - {0})
    grad, *sends = merge(
        lambda *refs: grad_kernel(inputs, *refs),
        [held[0]],
        [(rows, cols)] + [(1, cols + LANES * (len(first) - i)) for i in range(len(first) + 1)],
    )

    def send_wide(x, mask):
        return send_to(x, ("wide", "narrow"), wide * narrow, lambda i: i ^ mask)

    terms = [send_wide(x, mask * narrow ^ 1)[:, :cols] for x, mask in zip(sends, first)]
    grad = send_to(grad, group_axes, size, other)
    col_sum = tree(terms + [send_to(sends[-1], group_axes, size, other)])
    for masks in rounds:
        col_sum = tree([send_wide(col_sum, mask * narrow) for mask in masks] + [col_sum])
    new_col_state = BETA * col_state[None] + (1.0 - BETA) * (col_sum / rows_all)
    fixed = call(
        fixed_kernel,
        [(1, LANES)],
        [VMEM] * 2,
        weight, row_state[None],
        scratch=[pltpu.VMEM((1, LANES), jnp.float32)],
    )[0]

    single = dp * wide * narrow <= 64
    group = dp * narrow * (wide if single else 1)
    grad, message = call(
        column_kernel,
        [(rows, cols), (group, LANES)],
        [VMEM] * 3,
        new_col_state, grad, fixed,
    )
    if single:
        sums = lax.all_to_all(message, ("dp", "wide", "narrow"), 0, 0, tiled=True)
    else:
        sums = jnp.sum(lax.all_to_all(message, ("dp", "narrow"), 0, 0, tiled=True), axis=0, keepdims=True)
        sums = lax.all_to_all(jnp.broadcast_to(sums, (wide, LANES)), "wide", 0, 0, tiled=True)
    update, new_row_state = call(
        lambda *refs: final_kernel(rows_all, wide, narrow if single else 1, *refs),
        [(rows, cols), (1, rows)],
        [VMEM] * 2,
        sums, grad,
    )
    return (update, new_row_state[0], new_col_state[0])


def solution(mesh):
    dp, wide, narrow = (mesh.shape[axis] for axis in ("dp", "wide", "narrow"))

    def body(*args):
        return on_device(dp, wide, narrow, *args)

    return jax.shard_map(
        body,
        mesh=mesh,
        in_specs=(
            P(("dp", "narrow"), "wide", None),
            P("wide", ("dp", "narrow")),
            P("wide"),
            P(("dp", "narrow")),
        ),
        out_specs=(P("wide", ("dp", "narrow")), P("wide"), P(("dp", "narrow"))),
        check_vma=False,
    )
```

```python
import jax
import jax.numpy as jnp
from jax import lax
from jax.experimental import pallas as pl
from jax.experimental.pallas import tpu as pltpu
from jax.sharding import PartitionSpec as P

FF = 73728
STEP = 100
BETA = 1.0 - STEP ** (-0.8)
LANES = 128
PIECES = 4
VMEM = pl.BlockSpec(memory_space=pltpu.VMEM)
HBM = pl.BlockSpec(memory_space=pltpu.HBM)


def bits_of(size):
    return [1 << b for b in range(size.bit_length() - 1)]


def send_to(x, axes, size, target):
    return lax.ppermute(x, axes, [(i, target(i)) for i in range(size)])


def wide_masks(wide):
    bits = bits_of(wide)
    return [[sum(now)] * (len(now) - 1) + now[::-1] for now in (bits[i : i + 2] for i in range(0, len(bits), 2))]


def tree(terms):
    while len(terms) > 1:
        terms = [sum(terms[i : i + 2][1:], terms[i]) for i in range(0, len(terms), 2)]
    return terms[0]


def iota(rows, axis):
    return lax.broadcasted_iota(jnp.int32, (rows, LANES), axis)


def to_lanes(column, first):
    rows = column.shape[0]
    return jnp.sum(jnp.where(iota(rows, 1) == iota(rows, 0) + first, column, 0.0), axis=0, keepdims=True)


def call(kernel, out_shapes, in_specs, *args, scratch=()):
    return pl.pallas_call(
        kernel,
        out_shape=[jax.ShapeDtypeStruct(shape, jnp.float32) for shape in out_shapes],
        in_specs=in_specs,
        out_specs=[VMEM] * len(out_shapes),
        scratch_shapes=scratch,
        compiler_params=pltpu.CompilerParams(vmem_limit_bytes=32 << 20),
    )(*args)


class Blocks:
    def __init__(self, dp, narrow, cols):
        self.narrow, self.cols = narrow, cols
        self.masks = bits_of(dp * narrow)[1:]
        self.steps = len(self.masks)
        self.all = range(dp * narrow // 2)

    def mask(self, core, s):
        return self.masks[-1 - s] if core else self.masks[s]

    def home(self, t):
        return self.side(next((s for s in range(self.steps) if t >> s & 1), self.steps))

    def side(self, s):
        return (self.steps - s + 1) & 1

    def target(self, device, s, cross):
        return device ^ self.mask((device ^ self.side(s)) & 1, s) ^ cross

    def start(self, j, t):
        group = lax.axis_index("dp") * self.narrow + lax.axis_index("narrow")
        group = group ^ j
        reach = [sum(self.mask(core, s) for s in range(self.steps) if t >> s & 1) for core in range(2)]
        block = group ^ jnp.where(group % 2 == 1, reach[1], reach[0])
        return pl.multiple_of(block * self.cols, LANES)


def fetch_kernel(blocks, keys, part, out, raw, sem):
    spans, copies = [], []
    tiles = blocks.cols // LANES
    cuts = [tiles * i // PIECES * LANES for i in range(PIECES + 1)]
    for i, key in enumerate(keys):
        start = blocks.start(*key)
        for a, b in zip(cuts, cuts[1:]):
            spans.append(pl.ds(i * blocks.cols + a, b - a))
            source = part.at[:, pl.ds(pl.multiple_of(start + a, LANES), b - a)]
            copies.append(pltpu.make_async_copy(source, raw.at[:, spans[-1]], sem.at[len(copies)]))
    for i, copy in enumerate(copies):
        copy.start(priority=1 - i % 2)
    for copy, span in zip(copies, spans):
        copy.wait()
        out[:, span] = raw[:, span].astype(jnp.float32)


def load(blocks, refs, term):
    slot, at = term
    if slot == 0:
        return refs[0][:, pl.ds(blocks.start(*at), blocks.cols)].astype(jnp.float32)
    return refs[slot][:, at * blocks.cols : (at + 1) * blocks.cols]


def merge_kernel(blocks, plan, *refs):
    out = refs[-1]
    for i, terms in enumerate(plan):
        out[:, i * blocks.cols : (i + 1) * blocks.cols] = tree([load(blocks, refs, term) for term in terms])


def grad_kernel(inputs, blocks, plan, *refs):
    grad_out, *cols_out = refs[inputs:]
    cols = blocks.cols
    grad = tree([load(blocks, refs, term) for term in plan[0]])
    grad_out[...] = grad
    col = jnp.sum(grad * grad + 1e-30, axis=0, keepdims=True)
    for col_out in cols_out:
        col_out[:, :cols] = col
        if col_out.shape[1] > cols:
            col_out[:, cols:] = jnp.zeros((1, col_out.shape[1] - cols), jnp.float32)


def fixed_kernel(weight, row_state, out, line):
    rows = weight.shape[0]
    squares = []
    for at in range(0, weight.shape[1], LANES):
        piece = weight[:, at : at + LANES].astype(jnp.float32)
        squares.append(piece * piece)
    squares = jnp.sum(tree(squares), keepdims=True)
    line[...] = jnp.zeros_like(line)
    line[:, :rows] = row_state[...]
    first = jnp.logical_and(lax.axis_index("dp") == 0, lax.axis_index("narrow") == 0)
    state = jnp.where(first, pltpu.roll(line[...], 2 * rows, 1), 0.0)
    out[...] = jnp.where(iota(1, 1) == 3 * rows, squares, state)


def column_kernel(state, grad_in, fixed_in, grad_out, message_out):
    rows = grad_in.shape[0]
    row = jnp.sum(grad_in[...] * grad_in[...] + 1e-30, axis=1, keepdims=True)
    grad = grad_in[...] * lax.rsqrt(state[...])
    grad_out[...] = grad
    quot = jnp.sum(grad * grad, axis=1, keepdims=True)
    message = to_lanes(row, 0) + fixed_in[...] + to_lanes(quot, rows)
    message_out[...] = jnp.broadcast_to(message, message_out.shape)


def final_kernel(rows_all, wide, inner, sums_in, grad_in, update_out, row_out):
    rows = grad_in.shape[0]
    count = wide * inner
    total = tree([sums_in[i : i + count] for i in range(0, sums_in.shape[0], count)])
    total = tree([pltpu.roll(total, count - k, 0) if k else total for k in range(inner)])
    lane, layer = iota(count, 1), iota(count, 0)
    valid = jnp.logical_and(lane < rows, layer % inner == 0)
    state = pltpu.roll(total, LANES - 2 * rows, 1)
    quot = pltpu.roll(total, LANES - rows, 1)
    new = jnp.where(valid, BETA * state + (1.0 - BETA) * (total / FF), 1.0)
    update_sum = jnp.sum(jnp.where(valid, quot / new, 0.0), keepdims=True)
    weight_sum = jnp.sum(jnp.where(jnp.logical_and(lane == 3 * rows, layer % inner == 0), total, 0.0), keepdims=True)
    clip = jnp.maximum(1.0, jnp.sqrt(update_sum / (rows_all * FF)))
    weight_rms = jnp.maximum(0.001, jnp.sqrt(weight_sum / (rows_all * FF)))
    own = jnp.sum(jnp.where(layer == lax.axis_index("wide") * inner, new, 0.0), axis=0, keepdims=True)
    row_out[...] = own[:, :rows]
    column = jnp.sum(jnp.where(iota(rows, 1) == iota(rows, 0), own, 0.0), axis=1, keepdims=True)
    update_out[...] = grad_in[...] * (lax.rsqrt(column) * (weight_rms / clip))


def on_device(dp, wide, narrow, grad_parts, weight, row_state, col_state):
    part = grad_parts[0]
    rows, cols = weight.shape
    rows_all = rows * wide
    blocks = Blocks(dp, narrow, cols)
    group_axes = ("dp", "narrow")
    size = dp * narrow
    arrays = [part]
    held = {t: [(0, (blocks.home(t), t))] for t in blocks.all}

    def merge(kernel, sums, shapes):
        used = [0] + sorted({slot for terms in sums for slot, _ in terms} - {0}, reverse=True)
        plan = [[(used.index(slot), at) for slot, at in terms] for terms in sums]
        return call(lambda *refs: kernel(blocks, plan, *refs), shapes, [VMEM] * len(used), *[arrays[u] for u in used])

    def pack(sums):
        return merge(merge_kernel, sums, [(rows, len(sums) * cols)])[0]

    def fetch(keys):
        shape = (rows, len(keys) * cols)
        return call(
            lambda *refs: fetch_kernel(blocks, keys, *refs),
            [shape],
            [HBM],
            pltpu.with_memory_space_constraint(part, pltpu.HBM),
            scratch=[pltpu.VMEM(shape, part.dtype), pltpu.SemaphoreType.DMA((PIECES * len(keys),))],
        )[0]

    def receive(send, target):
        arrays.append(send_to(send, group_axes, size, target))
        return [(len(arrays) - 1, at) for at in range(send.shape[1] // cols)]

    def other(device):
        return device ^ 1

    def stages(s):
        groups = {}
        for t in blocks.all:
            if t & (2 << s) - 1 == 1 << s:
                cross = blocks.side(s) ^ blocks.home(t ^ 1 << s)
                groups.setdefault((t >> s == 1, 1 - cross), []).append(t)
        return [(ts, 1 - straight) for (_, straight), ts in sorted(groups.items())]

    even = [t for t in blocks.all if t and t % 2 == 0]
    groups = [ts for ts, _ in stages(0)] + [even, [0]]
    for i, ts in enumerate(group for group in groups if group):
        given = [(1 ^ blocks.home(t), t) for t in ts]
        send = pack([[(0, key)] for key in given]) if i else fetch(given)
        for t, term in zip(ts, receive(send, other)):
            held[t].append(term)
    for s in range(blocks.steps):
        for ts, cross in stages(s):
            send = pack([held.pop(t) for t in ts])
            for t, term in zip(ts, receive(send, lambda i: blocks.target(i, s, cross))):
                held[t ^ 1 << s].append(term)
    first, *rounds = wide_masks(wide)
    inputs = 1 + len({slot for slot, _ in held[0]} - {0})
    grad, *sends = merge(
        lambda *refs: grad_kernel(inputs, *refs),
        [held[0]],
        [(rows, cols)] + [(1, cols + LANES * (len(first) - i)) for i in range(len(first) + 1)],
    )

    def send_wide(x, mask):
        return send_to(x, ("wide", "narrow"), wide * narrow, lambda i: i ^ mask)

    terms = [send_wide(x, mask * narrow ^ 1)[:, :cols] for x, mask in zip(sends, first)]
    grad = send_to(grad, group_axes, size, other)
    col_sum = tree(terms + [send_to(sends[-1], group_axes, size, other)])
    for masks in rounds:
        col_sum = tree([send_wide(col_sum, mask * narrow) for mask in masks] + [col_sum])
    new_col_state = BETA * col_state[None] + (1.0 - BETA) * (col_sum / rows_all)
    fixed = call(
        fixed_kernel,
        [(1, LANES)],
        [VMEM] * 2,
        weight, row_state[None],
        scratch=[pltpu.VMEM((1, LANES), jnp.float32)],
    )[0]

    single = dp * wide * narrow <= 64
    group = dp * narrow * (wide if single else 1)
    grad, message = call(
        column_kernel,
        [(rows, cols), (group, LANES)],
        [VMEM] * 3,
        new_col_state, grad, fixed,
    )
    if single:
        sums = lax.all_to_all(message, ("dp", "wide", "narrow"), 0, 0, tiled=True)
    else:
        sums = jnp.sum(lax.all_to_all(message, ("dp", "narrow"), 0, 0, tiled=True), axis=0, keepdims=True)
        sums = lax.all_to_all(jnp.broadcast_to(sums, (wide, LANES)), "wide", 0, 0, tiled=True)
    update, new_row_state = call(
        lambda *refs: final_kernel(rows_all, wide, narrow if single else 1, *refs),
        [(rows, cols), (1, rows)],
        [VMEM] * 2,
        sums, grad,
    )
    return (update, new_row_state[0], new_col_state[0])


def solution(mesh):
    dp, wide, narrow = (mesh.shape[axis] for axis in ("dp", "wide", "narrow"))

    def body(*args):
        return on_device(dp, wide, narrow, *args)

    return jax.shard_map(
        body,
        mesh=mesh,
        in_specs=(
            P(("dp", "narrow"), "wide", None),
            P("wide", ("dp", "narrow")),
            P("wide"),
            P(("dp", "narrow")),
        ),
        out_specs=(P("wide", ("dp", "narrow")), P("wide"), P(("dp", "narrow"))),
        check_vma=False,
    )
```

```python
import jax
import jax.numpy as jnp
from jax import lax
from jax.experimental import pallas as pl
from jax.experimental.pallas import tpu as pltpu
from jax.sharding import PartitionSpec as P

FF = 73728
STEP = 100
BETA = 1.0 - STEP ** (-0.8)
LANES = 128
PIECES = 3
VMEM = pl.BlockSpec(memory_space=pltpu.VMEM)
HBM = pl.BlockSpec(memory_space=pltpu.HBM)


def bits_of(size):
    return [1 << b for b in range(size.bit_length() - 1)]


def send_to(x, axes, size, target):
    return lax.ppermute(x, axes, [(i, target(i)) for i in range(size)])


def wide_masks(wide):
    bits = bits_of(wide)
    return [[sum(now)] * (len(now) - 1) + now[::-1] for now in (bits[i : i + 2] for i in range(0, len(bits), 2))]


def tree(terms):
    while len(terms) > 1:
        terms = [sum(terms[i : i + 2][1:], terms[i]) for i in range(0, len(terms), 2)]
    return terms[0]


def iota(rows, axis):
    return lax.broadcasted_iota(jnp.int32, (rows, LANES), axis)


def to_lanes(column, first):
    rows = column.shape[0]
    return jnp.sum(jnp.where(iota(rows, 1) == iota(rows, 0) + first, column, 0.0), axis=0, keepdims=True)


def call(kernel, out_shapes, in_specs, *args, scratch=()):
    return pl.pallas_call(
        kernel,
        out_shape=[jax.ShapeDtypeStruct(shape, jnp.float32) for shape in out_shapes],
        in_specs=in_specs,
        out_specs=[VMEM] * len(out_shapes),
        scratch_shapes=scratch,
        compiler_params=pltpu.CompilerParams(vmem_limit_bytes=32 << 20),
    )(*args)


class Blocks:
    def __init__(self, dp, narrow, cols):
        self.narrow, self.cols = narrow, cols
        self.masks = bits_of(dp * narrow)[1:]
        self.steps = len(self.masks)
        self.all = range(dp * narrow // 2)

    def mask(self, core, s):
        return self.masks[-1 - s] if core else self.masks[s]

    def home(self, t):
        return self.side(next((s for s in range(self.steps) if t >> s & 1), self.steps))

    def side(self, s):
        return (self.steps - s + 1) & 1

    def target(self, device, s, cross):
        return device ^ self.mask((device ^ self.side(s)) & 1, s) ^ cross

    def start(self, j, t):
        group = lax.axis_index("dp") * self.narrow + lax.axis_index("narrow")
        group = group ^ j
        reach = [sum(self.mask(core, s) for s in range(self.steps) if t >> s & 1) for core in range(2)]
        block = group ^ jnp.where(group % 2 == 1, reach[1], reach[0])
        return pl.multiple_of(block * self.cols, LANES)


def fetch_kernel(blocks, keys, part, out, raw, sem):
    spans, copies = [], []
    tiles = blocks.cols // LANES
    cuts = [tiles * i // PIECES * LANES for i in range(PIECES + 1)]
    for i, key in enumerate(keys):
        start = blocks.start(*key)
        for a, b in zip(cuts, cuts[1:]):
            spans.append(pl.ds(i * blocks.cols + a, b - a))
            source = part.at[:, pl.ds(pl.multiple_of(start + a, LANES), b - a)]
            copies.append(pltpu.make_async_copy(source, raw.at[:, spans[-1]], sem.at[len(copies)]))
    for copy in copies:
        copy.start(priority=1)
    for copy, span in zip(copies, spans):
        copy.wait()
        out[:, span] = raw[:, span].astype(jnp.float32)


def load(blocks, refs, term):
    slot, at = term
    if slot == 0:
        return refs[0][:, pl.ds(blocks.start(*at), blocks.cols)].astype(jnp.float32)
    return refs[slot][:, at * blocks.cols : (at + 1) * blocks.cols]


def merge_kernel(blocks, plan, *refs):
    out = refs[-1]
    for i, terms in enumerate(plan):
        out[:, i * blocks.cols : (i + 1) * blocks.cols] = tree([load(blocks, refs, term) for term in terms])


def grad_kernel(inputs, blocks, plan, *refs):
    grad_out, *cols_out = refs[inputs:]
    cols = blocks.cols
    grad = tree([load(blocks, refs, term) for term in plan[0]])
    grad_out[...] = grad
    col = jnp.sum(grad * grad + 1e-30, axis=0, keepdims=True)
    for col_out in cols_out:
        col_out[:, :cols] = col
        if col_out.shape[1] > cols:
            col_out[:, cols:] = jnp.zeros((1, col_out.shape[1] - cols), jnp.float32)


def fixed_kernel(weight, row_state, out, line):
    rows = weight.shape[0]
    squares = []
    for at in range(0, weight.shape[1], LANES):
        piece = weight[:, at : at + LANES].astype(jnp.float32)
        squares.append(piece * piece)
    squares = jnp.sum(tree(squares), keepdims=True)
    line[...] = jnp.zeros_like(line)
    line[:, :rows] = row_state[...]
    first = jnp.logical_and(lax.axis_index("dp") == 0, lax.axis_index("narrow") == 0)
    state = jnp.where(first, pltpu.roll(line[...], 2 * rows, 1), 0.0)
    out[...] = jnp.where(iota(1, 1) == 3 * rows, squares, state)


def column_kernel(state, grad_in, fixed_in, grad_out, message_out):
    rows = grad_in.shape[0]
    row = jnp.sum(grad_in[...] * grad_in[...] + 1e-30, axis=1, keepdims=True)
    grad = grad_in[...] * lax.rsqrt(state[...])
    grad_out[...] = grad
    quot = jnp.sum(grad * grad, axis=1, keepdims=True)
    message = to_lanes(row, 0) + fixed_in[...] + to_lanes(quot, rows)
    message_out[...] = jnp.broadcast_to(message, message_out.shape)


def final_kernel(rows_all, wide, inner, sums_in, grad_in, update_out, row_out):
    rows = grad_in.shape[0]
    count = wide * inner
    total = tree([sums_in[i : i + count] for i in range(0, sums_in.shape[0], count)])
    total = tree([pltpu.roll(total, count - k, 0) if k else total for k in range(inner)])
    lane, layer = iota(count, 1), iota(count, 0)
    valid = jnp.logical_and(lane < rows, layer % inner == 0)
    state = pltpu.roll(total, LANES - 2 * rows, 1)
    quot = pltpu.roll(total, LANES - rows, 1)
    new = jnp.where(valid, BETA * state + (1.0 - BETA) * (total / FF), 1.0)
    update_sum = jnp.sum(jnp.where(valid, quot / new, 0.0), keepdims=True)
    weight_sum = jnp.sum(jnp.where(jnp.logical_and(lane == 3 * rows, layer % inner == 0), total, 0.0), keepdims=True)
    clip = jnp.maximum(1.0, jnp.sqrt(update_sum / (rows_all * FF)))
    weight_rms = jnp.maximum(0.001, jnp.sqrt(weight_sum / (rows_all * FF)))
    own = jnp.sum(jnp.where(layer == lax.axis_index("wide") * inner, new, 0.0), axis=0, keepdims=True)
    row_out[...] = own[:, :rows]
    column = jnp.sum(jnp.where(iota(rows, 1) == iota(rows, 0), own, 0.0), axis=1, keepdims=True)
    update_out[...] = grad_in[...] * (lax.rsqrt(column) * (weight_rms / clip))


def on_device(dp, wide, narrow, grad_parts, weight, row_state, col_state):
    part = grad_parts[0]
    rows, cols = weight.shape
    rows_all = rows * wide
    blocks = Blocks(dp, narrow, cols)
    group_axes = ("dp", "narrow")
    size = dp * narrow
    arrays = [part]
    held = {t: [(0, (blocks.home(t), t))] for t in blocks.all}

    def merge(kernel, sums, shapes):
        used = [0] + sorted({slot for terms in sums for slot, _ in terms} - {0}, reverse=True)
        plan = [[(used.index(slot), at) for slot, at in terms] for terms in sums]
        return call(lambda *refs: kernel(blocks, plan, *refs), shapes, [VMEM] * len(used), *[arrays[u] for u in used])

    def pack(sums):
        return merge(merge_kernel, sums, [(rows, len(sums) * cols)])[0]

    def fetch(keys):
        shape = (rows, len(keys) * cols)
        return call(
            lambda *refs: fetch_kernel(blocks, keys, *refs),
            [shape],
            [HBM],
            pltpu.with_memory_space_constraint(part, pltpu.HBM),
            scratch=[pltpu.VMEM(shape, part.dtype), pltpu.SemaphoreType.DMA((PIECES * len(keys),))],
        )[0]

    def receive(send, target):
        arrays.append(send_to(send, group_axes, size, target))
        return [(len(arrays) - 1, at) for at in range(send.shape[1] // cols)]

    def other(device):
        return device ^ 1

    def stages(s):
        groups = {}
        for t in blocks.all:
            if t & (2 << s) - 1 == 1 << s:
                cross = blocks.side(s) ^ blocks.home(t ^ 1 << s)
                groups.setdefault((t >> s == 1, 1 - cross), []).append(t)
        return [(ts, 1 - straight) for (_, straight), ts in sorted(groups.items())]

    even = [t for t in blocks.all if t and t % 2 == 0]
    groups = [ts for ts, _ in stages(0)] + [even, [0]]
    for i, ts in enumerate(group for group in groups if group):
        given = [(1 ^ blocks.home(t), t) for t in ts]
        send = pack([[(0, key)] for key in given]) if i else fetch(given)
        for t, term in zip(ts, receive(send, other)):
            held[t].append(term)
    for s in range(blocks.steps):
        for ts, cross in stages(s):
            send = pack([held.pop(t) for t in ts])
            for t, term in zip(ts, receive(send, lambda i: blocks.target(i, s, cross))):
                held[t ^ 1 << s].append(term)
    first, *rounds = wide_masks(wide)
    inputs = 1 + len({slot for slot, _ in held[0]} - {0})
    grad, *sends = merge(
        lambda *refs: grad_kernel(inputs, *refs),
        [held[0]],
        [(rows, cols)] + [(1, cols + LANES * (len(first) - i)) for i in range(len(first) + 1)],
    )

    def send_wide(x, mask):
        return send_to(x, ("wide", "narrow"), wide * narrow, lambda i: i ^ mask)

    terms = [send_wide(x, mask * narrow ^ 1)[:, :cols] for x, mask in zip(sends, first)]
    grad = send_to(grad, group_axes, size, other)
    col_sum = tree(terms + [send_to(sends[-1], group_axes, size, other)])
    for masks in rounds:
        col_sum = tree([send_wide(col_sum, mask * narrow) for mask in masks] + [col_sum])
    new_col_state = BETA * col_state[None] + (1.0 - BETA) * (col_sum / rows_all)
    fixed = call(
        fixed_kernel,
        [(1, LANES)],
        [VMEM] * 2,
        weight, row_state[None],
        scratch=[pltpu.VMEM((1, LANES), jnp.float32)],
    )[0]

    single = dp * wide * narrow <= 64
    group = dp * narrow * (wide if single else 1)
    grad, message = call(
        column_kernel,
        [(rows, cols), (group, LANES)],
        [VMEM] * 3,
        new_col_state, grad, fixed,
    )
    if single:
        sums = lax.all_to_all(message, ("dp", "wide", "narrow"), 0, 0, tiled=True)
    else:
        sums = jnp.sum(lax.all_to_all(message, ("dp", "narrow"), 0, 0, tiled=True), axis=0, keepdims=True)
        sums = lax.all_to_all(jnp.broadcast_to(sums, (wide, LANES)), "wide", 0, 0, tiled=True)
    update, new_row_state = call(
        lambda *refs: final_kernel(rows_all, wide, narrow if single else 1, *refs),
        [(rows, cols), (1, rows)],
        [VMEM] * 2,
        sums, grad,
    )
    return (update, new_row_state[0], new_col_state[0])


def solution(mesh):
    dp, wide, narrow = (mesh.shape[axis] for axis in ("dp", "wide", "narrow"))

    def body(*args):
        return on_device(dp, wide, narrow, *args)

    return jax.shard_map(
        body,
        mesh=mesh,
        in_specs=(
            P(("dp", "narrow"), "wide", None),
            P("wide", ("dp", "narrow")),
            P("wide"),
            P(("dp", "narrow")),
        ),
        out_specs=(P("wide", ("dp", "narrow")), P("wide"), P(("dp", "narrow"))),
        check_vma=False,
    )
```
